128 devices in a mesh: fsdp: 4 (over z_hi, core), blk: 32 (over y, z_lo, x).
Axes of the slice: x: 4, y: 4, z: 4 (z_hi: 2, z_lo: 2; z = z_hi * 2 + z_lo), core: 2. Of those that a mesh axis runs over, the one named last changes fastest.
Arguments:
- query_nope: bfloat16 [4, 4096, 1024], P('fsdp', 'blk'), may hold values from -6 to 6
- query_rope: bfloat16 [4, 4096, 512], P('fsdp', 'blk'), may hold values from -500 to 500
- latent: bfloat16 [4, 4096, 576], P('fsdp', 'blk'), may hold values from -5 to 5
- grad_out: bfloat16 [4, 4096, 1024], P('fsdp', 'blk'), may hold values from -6 to 6
- w_up: bfloat16 [512, 2048], P('fsdp'), may hold values from -0.5 to 0.5
- block_order: int32 [32, 2], replicated, may hold values from 0 to 63, as said below
Outputs:
- grad_query_nope: bfloat16 [4, 4096, 1024], P('fsdp', 'blk')
- grad_query_rope: bfloat16 [4, 4096, 512], P('fsdp', 'blk')
- grad_latent: bfloat16 [4, 4096, 576], P('fsdp', 'blk')
- grad_up: float32 [512, 2048], P(('fsdp', 'blk'))
The draws below stay inside these ranges and needn't reach their ends.
Inputs may be any that keep to these rules, and one draw needn't show every extreme that they name: block_order[i, 1] = 63 - block_order[i, 0] and block_order[i, 0] < 32; every block 0 to 63 is held by exactly one device.
All inputs are finite; a program needn't handle non-finite values.
Results may differ from the reference program's by a relative error of at most 0.013.
Values may be sent and summed in bfloat16 or wider, within the bound.
A program may use at most 128 MiB of HBM per device.

```python
import math
import jax
import jax.numpy as jnp
from jax import lax

HEADS = 8
NOPE_DIM = 128
ROPE_DIM = 64
VALUE_DIM = 128
LATENT = 512
HALF_BLOCK = 64
SEQ_LEN = 4096
N_FSDP = 4
N_BLK = 32


def rope_keys(key, chance):
    normal_keys = jnp.clip(jax.random.normal(jax.random.fold_in(key, 11), (N_FSDP, SEQ_LEN, ROPE_DIM), jnp.float32), -5.0, 5.0)
    offsets = jnp.arange(SEQ_LEN) % HALF_BLOCK
    chosen_rows = jax.random.bernoulli(jax.random.fold_in(key, 13), chance, (N_FSDP, SEQ_LEN)) & (offsets != 0)[None, :]
    before_rows = jnp.roll(chosen_rows, -1, axis=1)
    rotary_keys = jnp.where(before_rows[:, :, None], jnp.roll(normal_keys, -1, axis=1), normal_keys)
    return rotary_keys


def draw_latent(key, part):
    rotary_keys = rope_keys(key, 0.0)
    key = jax.random.fold_in(key, 17)
    values = jnp.clip(jax.random.normal(key, (N_FSDP, SEQ_LEN, LATENT), jnp.float32), -5.0, 5.0)
    return jnp.concatenate([values, rotary_keys], axis=-1).astype(jnp.bfloat16)


def draw_query_rope(key, part):
    key = jax.random.fold_in(key, 19)
    queries = jnp.clip(jax.random.normal(key, (N_FSDP, SEQ_LEN, HEADS, ROPE_DIM), jnp.float32), -5.0, 5.0)
    return queries.reshape(N_FSDP, SEQ_LEN, HEADS * ROPE_DIM).astype(jnp.bfloat16)


def draw_block_order(key, part):
    key = jax.random.fold_in(key, 3)
    first = jax.random.permutation(key, N_BLK).astype(jnp.int32)
    return jnp.stack([first, 2 * N_BLK - 1 - first], axis=1).astype(jnp.int32)


def level_of(rng, extent, shards, smallest, top_value):
    def one(dim, shards_of):
        heights = jax.random.uniform(jax.random.fold_in(jax.random.fold_in(rng, 6), dim), (shards_of,), jnp.float32, smallest / len(shards), top_value / len(shards))
        return jnp.repeat(jnp.exp(heights), extent[dim] // shards_of).reshape((-1,) + (1,) * (len(extent) - dim - 1))

    gain = one(*shards[0])
    for cut in shards[1:]:
        gain = gain * one(*cut)
    return gain


def centred(key, extent, scale, reach, pieces=(), kind=jnp.bfloat16):
    drawn = scale * jax.random.normal(key, extent, jnp.float32)
    if pieces:
        drawn = drawn * level_of(key, extent, pieces, -0.22, 0.18)
    return jnp.clip(drawn, -reach, reach).astype(kind)


def setup_inputs(seed: int = 0) -> dict:
    splits = jax.random.split(jax.random.key(seed), 7)
    return {
        "query_nope": centred(splits[0], (N_FSDP, SEQ_LEN, HEADS * NOPE_DIM), 1.0, 6.0, ((0, 4), (1, 32))),
        "query_rope": draw_query_rope(jax.random.fold_in(splits[6], 71), 0),
        "latent": draw_latent(jax.random.fold_in(splits[6], 71), 0),
        "grad_out": centred(splits[3], (N_FSDP, SEQ_LEN, HEADS * VALUE_DIM), 1.0, 6.0, ((0, 4), (1, 32))),
        "w_up": centred(splits[4], (LATENT, HEADS * (NOPE_DIM + VALUE_DIM)), NOPE_DIM ** -0.5, 0.5, ((0, 4),)),
        "block_order": draw_block_order(jax.random.fold_in(splits[6], 71), 0),
    }


NEG_FILL = -1e+30

def low_copy(values):
    return lax.optimization_barrier(values.astype(jnp.bfloat16)).astype(jnp.float32)

def one_sequence(query_nope, query_rope, latent, grad_out, w_key, w_value, positions):
    scale = 1.0 / math.sqrt(NOPE_DIM + ROPE_DIM)
    width = LATENT + ROPE_DIM
    nope_rows = query_nope.astype(jnp.float32).reshape(SEQ_LEN, HEADS, NOPE_DIM)
    absorbed = low_copy(jnp.einsum('thn,jhn->thj', nope_rows, w_key))
    rope_rows = query_rope.astype(jnp.float32).reshape(SEQ_LEN, HEADS, ROPE_DIM)
    query_full = jnp.concatenate([absorbed, rope_rows], axis=-1)
    grad_heads = grad_out.astype(jnp.float32).reshape(SEQ_LEN, HEADS, VALUE_DIM)
    grad_absorbed = low_copy(jnp.einsum('thv,jhv->thj', grad_heads, w_value))
    key_rows = latent.astype(jnp.float32)
    latent_rows = key_rows[:, :LATENT]
    block_rows = math.gcd(SEQ_LEN, 512)
    count = SEQ_LEN // block_rows

    def block_step(key_terms, number):
        start = number * block_rows
        query_block = lax.dynamic_slice_in_dim(query_full, start, block_rows, 0)
        grad_block = lax.dynamic_slice_in_dim(grad_absorbed, start, block_rows, 0)
        query_pos = lax.dynamic_slice_in_dim(positions, start, block_rows, 0)
        scores = jnp.einsum('thk,uk->htu', query_block, key_rows) * scale
        allowed = positions[None, None, :] <= query_pos[None, :, None]
        scores = jnp.where(allowed, scores, NEG_FILL)
        peak = lax.optimization_barrier(jnp.max(scores, axis=-1, keepdims=True))
        total = lax.optimization_barrier(jnp.sum(jnp.where(allowed, jnp.exp(scores - peak), 0.0), axis=-1, keepdims=True))
        norm_log = peak + jnp.log(total)
        probs = jnp.where(allowed, jnp.exp(scores - norm_log), 0.0)
        grad_probs = jnp.einsum('thj,uj->htu', grad_block, latent_rows)
        centre = lax.optimization_barrier(jnp.sum(probs * grad_probs, axis=-1, keepdims=True))
        grad_scores = probs * (grad_probs - centre)
        probs_low = low_copy(probs)
        grad_low = low_copy(grad_scores)
        out_latent = jnp.einsum('htu,uj->thj', probs_low, latent_rows)
        grad_full = jnp.einsum('htu,uk->thk', grad_low, key_rows) * scale
        term = jnp.einsum('htu,thk->uk', grad_low, query_block) * scale
        value_term = jnp.einsum('htu,thj->uj', probs_low, grad_block)
        term = term + jnp.pad(value_term, ((0, 0), (0, ROPE_DIM)))
        return (key_terms + term, (grad_full, out_latent))
    start_terms = jnp.zeros((SEQ_LEN, width), jnp.float32)
    key_terms, (grad_full, out_latent) = lax.scan(block_step, start_terms, jnp.arange(count, dtype=jnp.int32))
    grad_full = grad_full.reshape(SEQ_LEN, HEADS, width)
    out_latent = out_latent.reshape(SEQ_LEN, HEADS, LATENT)
    grad_abs_low = low_copy(grad_full[:, :, :LATENT])
    grad_rope = grad_full[:, :, LATENT:].astype(jnp.bfloat16).reshape(SEQ_LEN, HEADS * ROPE_DIM)
    grad_nope = jnp.einsum('thj,jhn->thn', grad_abs_low, w_key).astype(jnp.bfloat16).reshape(SEQ_LEN, HEADS * NOPE_DIM)
    out_low = low_copy(out_latent)
    grad_key_w = jnp.einsum('thj,thn->jhn', grad_abs_low, nope_rows).reshape(LATENT, HEADS * NOPE_DIM)
    grad_value_w = jnp.einsum('thj,thv->jhv', out_low, grad_heads).reshape(LATENT, HEADS * VALUE_DIM)
    weight_terms = jnp.concatenate([grad_key_w, grad_value_w], axis=1)
    return (grad_nope, grad_rope, key_terms.astype(jnp.bfloat16), weight_terms)

def reference(query_nope, query_rope, latent, grad_out, w_up, block_order):
    offsets = jnp.arange(HALF_BLOCK, dtype=jnp.int32)
    positions = (block_order[:, :, None] * HALF_BLOCK + offsets[None, None, :]).reshape(SEQ_LEN).astype(jnp.int32)
    weights = w_up.astype(jnp.float32)
    w_key = weights[:, :HEADS * NOPE_DIM].reshape(LATENT, HEADS, NOPE_DIM)
    w_value = weights[:, HEADS * NOPE_DIM:].reshape(LATENT, HEADS, VALUE_DIM)
    nope_list = []
    rope_list = []
    latent_list = []
    grad_up = jnp.zeros((LATENT, HEADS * (NOPE_DIM + VALUE_DIM)), jnp.float32)
    for number in range(N_FSDP):
        grad_nope, grad_rope, grad_keys, weight_terms = one_sequence(query_nope[number], query_rope[number], latent[number], grad_out[number], w_key, w_value, positions)
        nope_list.append(grad_nope)
        rope_list.append(grad_rope)
        latent_list.append(grad_keys)
        grad_up = grad_up + weight_terms
    return (jnp.stack(nope_list), jnp.stack(rope_list), jnp.stack(latent_list), grad_up)
```

```python
import functools
import math

import jax
import jax.numpy as jnp
from jax import lax
from jax.experimental import pallas as pl
from jax.experimental.pallas import tpu as pltpu
from jax.sharding import PartitionSpec as P

HEADS = 8
LATENT = 512
SCALE = 1.0 / math.sqrt(192.0)
NEG_FILL = -1e30
F32 = jnp.float32
BF16 = jnp.bfloat16
MESH = pl.DeviceIdType.MESH
COPIES = 112


def mm(a, b):
    return lax.dot_general(a, b, (((1,), (0,)), ((), ())), preferred_element_type=F32)


def mm_nt(a, b):
    return lax.dot_general(a, b, (((1,), (1,)), ((), ())), preferred_element_type=F32)


def add_into(ref, *others):
    total = ref[...].astype(F32)
    for other in others:
        total = total + other[...].astype(F32)
    ref[...] = total.astype(BF16)


def kernel(
    order, lat, nope_o, rope_o, gout_o, w_own,
    gn_out, gr_out, gl_out, gu_out,
    kbuf, keys, keys_t, nope_p, rope_p, gout_p, w_all, wk_t,
    query, grad, probs, gprob, gscore, peaks, peak, total, centre, stat_s, stat_r,
    dq_t, out_t, gn_own, gn_send, gn_recv, ro_recv,
    dkb, ra1, ra2, ra3, ra4, rb1, rb2, rb3, rb4,
    up, uc, uzs, uz, us1, upr, us2, uyr, us3, uxr,
    send, recv,
):
    f = lax.axis_index("fsdp")
    blk = lax.axis_index("blk")
    x, zl, y = blk % 4, (blk // 4) % 2, blk // 8
    xp, xm, x2 = (x + 1) % 4, (x + 3) % 4, (x + 2) % 4
    yp, ym, y2 = (y + 1) % 4, (y + 3) % 4, (y + 2) % 4
    f1 = f + 1 - 2 * (f % 2)
    f2 = (f + 2) % 4
    f3 = (f1 + 2) % 4

    def at(yy, xx):
        return {"blk": (yy * 2 + zl) * 4 + xx}

    to_xp, to_xm, to_x2 = at(y, xp), at(y, xm), at(y, x2)
    to_yp, to_ym, to_y2 = at(yp, x), at(ym, x), at(y2, x)
    to_pair = {"blk": blk + 4 - 8 * zl}
    to_core = {"fsdp": f1}
    to_far = {"fsdp": f2, "blk": blk + 4 - 8 * zl}

    made = {}

    def define(name, src, dst, device):
        number = len(made)
        made[name] = lambda: pltpu.make_async_remote_copy(
            src_ref=src(), dst_ref=dst(), send_sem=send.at[number], recv_sem=recv.at[number],
            device_id=device, device_id_type=MESH,
        )

    def start(*names):
        for name in names:
            made[name]().start()

    def wait(*names):
        for name in names:
            made[name]().wait_recv()

    def key_part(yy, xx, first, count):
        return lambda: kbuf.at[yy * 4 + xx, pl.ds(first, count)]

    def same(name, part, device):
        define(name, part, part, device)

    for name, first, count, cut, swap in (("a", 0, 80, 48, False), ("b", 80, 64, 32, True)):
        def part(dy, dx, first=first, count=count, swap=swap):
            if swap:
                dy, dx = dx, dy
            return key_part((y + dy) % 4, (x + dx) % 4, first, count)

        ip, im, jp, jm = (to_yp, to_ym, to_xp, to_xm) if swap else (to_xp, to_xm, to_yp, to_ym)
        same(name + "1", part(0, 0), ip)
        same(name + "2", part(0, 0), im)
        same(name + "3", part(0, 0), jp)
        same(name + "4", part(0, 0), jm)
        same(name + "5", part(0, 3, first, cut), ip)
        same(name + "6", part(0, 1, first + cut, count - cut), im)
        same(name + "7", part(0, 3), jp)
        same(name + "8", part(0, 3), jm)
        same(name + "9", part(0, 1), jp)
        same(name + "10", part(0, 1), jm)
        same(name + "11", part(0, 2), jp)
        same(name + "12", part(0, 2), jm)
        same(name + "13", part(3, 0), jp)
        same(name + "14", part(3, 3), jp)
        same(name + "15", part(1, 1), jm)
        same(name + "16", part(1, 2), jm)

    define("qn", lambda: nope_o, lambda: nope_p, to_pair)
    define("qr", lambda: rope_o, lambda: rope_p, to_pair)
    define("qg", lambda: gout_o, lambda: gout_p, to_pair)
    define("w1", lambda: w_own, lambda: w_all.at[f], to_core)
    define("w2", lambda: w_own, lambda: w_all.at[f], to_far)
    define("w3", lambda: w_all.at[f2], lambda: w_all.at[f2], to_core)
    define("st", lambda: stat_s, lambda: stat_r, to_pair)
    define("gn", lambda: gn_send, lambda: gn_recv, to_pair)
    define("ro1", lambda: dq_t.at[1, pl.ds(512, 64)], lambda: ro_recv.at[0], to_pair)
    define("ro3", lambda: dq_t.at[3, pl.ds(512, 64)], lambda: ro_recv.at[1], to_pair)

    def terms(yy, xx, first, count):
        return lambda: dkb.at[yy, xx, pl.ds(first, count)]

    def term_rows(yy, x_first, x_count):
        return lambda: dkb.at[yy, pl.ds(x_first, x_count), pl.ds(0, 80)]

    define("A1p", term_rows(y2, 0, 2), lambda: ra1.at[0], to_yp)
    define("A1m", term_rows(y2, 2, 2), lambda: ra1.at[1], to_ym)
    define("A2p", term_rows(yp, 0, 4), lambda: ra2.at[0], to_yp)
    define("A2m", term_rows(ym, 0, 4), lambda: ra2.at[1], to_ym)
    define("A3p", terms(y, x2, 0, 48), lambda: ra3.at[pl.ds(0, 48)], to_xp)
    define("A3m", terms(y, x2, 48, 32), lambda: ra3.at[pl.ds(48, 32)], to_xm)
    define("A4p", terms(y, xp, 0, 80), lambda: ra4.at[0], to_xp)
    define("A4m", terms(y, xm, 0, 80), lambda: ra4.at[1], to_xm)
    turns = (y2, yp, ym, y)
    for i in range(4):
        define(f"B1{i}", terms(turns[i], x2, 80, 64), lambda i=i: rb1.at[i], to_xp if i % 2 == 0 else to_xm)
        define(f"B2p{i}", terms(turns[i], xp, 80, 64), lambda i=i: rb2.at[i, 0], to_xp)
        define(f"B2m{i}", terms(turns[i], xm, 80, 64), lambda i=i: rb2.at[i, 1], to_xm)
    define("B3p", terms(y2, x, 80, 32), lambda: rb3.at[0], to_yp)
    define("B3m", terms(y2, x, 112, 32), lambda: rb3.at[1], to_ym)
    define("B4p", terms(yp, x, 80, 64), lambda: rb4.at[0], to_yp)
    define("B4m", terms(ym, x, 80, 64), lambda: rb4.at[1], to_ym)

    for i in range(2):
        define(f"C0{i}", lambda i=i: up.at[i, f1], lambda i=i: uc.at[i, 0], to_core)
        define(f"C1{i}", lambda i=i: up.at[i, f3], lambda i=i: uc.at[i, 1], to_core)
        define(f"Z{i}", lambda i=i: uzs.at[i], lambda i=i: uz.at[i], to_far)
        define(f"P{i}", lambda i=i: us1.at[i, :, 1 - zl], lambda i=i: upr.at[i], to_pair)
        define(f"Yp{i}", lambda i=i: us2.at[i, yp], lambda i=i: uyr.at[i, 0], to_yp)
        define(f"Ym{i}", lambda i=i: us2.at[i, ym], lambda i=i: uyr.at[i, 1], to_ym)
        define(f"Y2{i}", lambda i=i: us2.at[i, y2], lambda i=i: uyr.at[i, 2], to_y2)
        define(f"Xp{i}", lambda i=i: us3.at[i], lambda i=i: uxr.at[i, 0], to_xp)
        define(f"Xm{i}", lambda i=i: us3.at[i], lambda i=i: uxr.at[i, 1], to_xm)
        define(f"X2{i}", lambda i=i: us3.at[i], lambda i=i: uxr.at[i, 2], to_x2)

    mine = y * 4 + x
    kbuf[mine, 0:64] = lat[0:64, 0:512]
    kbuf[mine, 80:144] = lat[64:128, 0:512]
    kbuf[mine, 64:80] = jnp.concatenate([lat[s * 16 : s * 16 + 16, 512:576] for s in range(8)], axis=1)
    barrier = pltpu.get_barrier_semaphore()
    partners = (to_xp, to_xm, to_x2, to_yp, to_ym, to_y2, to_pair, to_core, to_far)
    for partner in partners:
        pl.semaphore_signal(barrier, inc=1, device_id=partner, device_id_type=MESH)
    pl.semaphore_wait(barrier, len(partners))

    start("w2", "qn", "a1", "a2", "b1", "b2", "a3", "a4", "b3", "b4", "w1", "qg", "qr")
    w_all[f] = w_own[...]
    for g in range(4):
        query[g, :, 512:640] = jnp.zeros((512, 128), BF16)
    for t in range(8):
        keys[t, :, 512:640] = jnp.zeros((256, 128), BF16)
    for name in ("a", "b"):
        wait(name + "1")
        start(name + "5", name + "7", name + "8")
    for name in ("a", "b"):
        wait(name + "2")
        start(name + "6", name + "9", name + "10")
    for name in ("a", "b"):
        wait(name + "5", name + "6")
        start(name + "11", name + "12")
    for name in ("a", "b"):
        wait(name + "3")
        start(name + "13")
    for name in ("a", "b"):
        wait(name + "7")
        start(name + "14")
    for name in ("a", "b"):
        wait(name + "10")
        start(name + "15")
    for name in ("a", "b"):
        wait(name + "12")
        start(name + "16")

    def project(shard, nope, gout, low, high):
        columns = pl.ds(pl.multiple_of(shard * 128, 128), 128)

        def head(h, _):
            lanes = pl.ds(pl.multiple_of(h * 128, 128), 128)
            value_lanes = pl.ds(pl.multiple_of(1024 + h * 128, 128), 128)
            rows = pl.ds(pl.multiple_of(h * 64, 64), 64)
            a = mm_nt(nope[:, lanes], w_all[shard, :, lanes]).astype(BF16)
            query[low, rows, columns] = a[:64]
            query[high, rows, columns] = a[64:]
            b = mm_nt(gout[:, lanes], w_all[shard, :, value_lanes]).astype(BF16)
            grad[low, rows, columns] = b[:64]
            grad[high, rows, columns] = b[64:]
            return 0

        lax.fori_loop(0, HEADS, head, 0)

    def place_rope(rope, low, high):
        for h in range(HEADS):
            part = rope[:, h * 64 : h * 64 + 64]
            query[low, h * 64 : h * 64 + 64, 512:576] = part[:64]
            query[high, h * 64 : h * 64 + 64, 512:576] = part[64:]

    project(f, nope_o, gout_o, 2, 0)
    place_rope(rope_o, 2, 0)
    wait("w1")
    project(f1, nope_o, gout_o, 2, 0)
    wait("w2")
    start("w3")
    project(f2, nope_o, gout_o, 2, 0)
    wait("qn", "qg", "qr")
    place_rope(rope_p, 3, 1)
    project(f, nope_p, gout_p, 3, 1)
    project(f1, nope_p, gout_p, 3, 1)
    project(f2, nope_p, gout_p, 3, 1)
    wait("w3")
    project(f3, nope_o, gout_o, 2, 0)
    project(f3, nope_p, gout_p, 3, 1)

    for name in ("a", "b"):
        wait(*(name + n for n in ("4", "8", "9", "11", "13", "14", "15", "16")))

    def assemble(p, _):
        yy, xx = p // 4, p % 4
        rows = pl.ds(pl.multiple_of(xx * 64, 64), 64)
        keys[yy, rows, 0:512] = kbuf[p, 0:64]
        keys[4 + yy, rows, 0:512] = kbuf[p, 80:144]
        packed = kbuf[p, 64:80]
        low = jnp.concatenate([packed[:, s * 64 : s * 64 + 64] for s in range(4)], axis=0)
        high = jnp.concatenate([packed[:, s * 64 : s * 64 + 64] for s in range(4, 8)], axis=0)
        keys[yy, rows, 512:576] = low
        keys[4 + yy, rows, 512:576] = high
        return 0

    lax.fori_loop(0, 16, assemble, 0)

    peak[...] = jnp.full((4, 1, 512), NEG_FILL, F32)
    total[...] = jnp.zeros((4, 1, 512), F32)
    centre[...] = jnp.zeros((4, 1, 512), F32)
    own_first = order[blk, 0]
    pair_first = order[blk + 4 - 8 * zl, 0]
    relative = lax.broadcasted_iota(jnp.int32, (64, 512), 0) - lax.broadcasted_iota(jnp.int32, (64, 512), 1) % 64

    def visit(t, g, high, masked):
        tile = 4 + t if high else t
        slot = 16 + g * 4 + t if high else g * 4 + t
        scores = mm_nt(keys[tile], query[g])
        grad_probs = mm_nt(keys[tile, :, 0:512], grad[g])
        if masked:
            first = jnp.where(g % 2 == 0, own_first, pair_first)
            block = 63 - first if high else first
            parts = []
            for xx in range(4):
                key_first = order[(t * 2 + zl) * 4 + xx, 0]
                key_block = 63 - key_first if high else key_first
                parts.append(relative <= (block - key_block) * 64)
            allowed = jnp.concatenate(parts, axis=0)
            scores = jnp.where(allowed, scores, NEG_FILL)
        old = peak[g]
        new = jnp.maximum(old, jnp.max(scores, axis=0, keepdims=True))
        weights = jnp.exp((scores - new) * SCALE)
        if masked:
            weights = jnp.where(allowed, weights, 0.0)
        factor = jnp.exp((old - new) * SCALE)
        total[g] = total[g] * factor + jnp.sum(weights, axis=0, keepdims=True)
        centre[g] = centre[g] * factor + jnp.sum(weights * grad_probs, axis=0, keepdims=True)
        peak[g] = new
        probs[slot] = weights.astype(BF16)
        gprob[slot] = grad_probs
        peaks[slot] = new

    def open_low(i, _):
        visit(i // 2, i % 2, False, False)
        return 0

    def masked_low(i, _):
        visit(i // 2, 2 + i % 2, False, True)
        return 0

    def masked_high(i, _):
        visit(i // 2, i % 2, True, True)
        return 0

    lax.fori_loop(0, 8, open_low, 0)
    lax.fori_loop(0, 8, masked_low, 0)
    lax.fori_loop(0, 8, masked_high, 0)

    for g in range(4):
        stat_s[g, 0:1] = peak[g]
        stat_s[g, 1:2] = total[g]
        stat_s[g, 2:3] = centre[g]
    start("st")
    for t in range(8):
        keys_t[:, t * 256 : t * 256 + 256] = jnp.transpose(keys[t])
    for s in range(4):
        wk_t[:, s * 128 : s * 128 + 128] = jnp.transpose(w_all[s, :, 0:1024])
    wait("st")
    for g in range(4):
        other = g + 1 - 2 * (g % 2)
        here, there = stat_s[g], stat_r[other]
        new = jnp.maximum(here[0:1], there[0:1])
        f_here = jnp.exp((here[0:1] - new) * SCALE)
        f_there = jnp.exp((there[0:1] - new) * SCALE)
        norm = here[1:2] * f_here + there[1:2] * f_there
        peak[g] = new
        total[g] = norm
        centre[g] = (here[2:3] * f_here + there[2:3] * f_there) / norm

    def normalise(slot, g):
        factor = jnp.exp((peaks[slot] - peak[g]) * SCALE) / total[g]
        p = probs[slot].astype(F32) * factor
        probs[slot] = p.astype(BF16)
        gscore[slot] = (p * (gprob[slot] - centre[g]) * SCALE).astype(BF16)

    def normalise_low(i, _):
        normalise(i, i // 4)
        return 0

    def normalise_high(i, _):
        normalise(16 + i, i // 4)
        return 0

    lax.fori_loop(0, 16, normalise_low, 0)
    lax.fori_loop(0, 8, normalise_high, 0)

    def low_rows(ref, g):
        return ref[pl.ds(g * 4, 4)].reshape(1024, 512)

    def all_rows(ref, g):
        return jnp.concatenate([low_rows(ref, g), ref[pl.ds(16 + g * 4, 4)].reshape(1024, 512)], axis=0)

    def out_high(g, _):
        out_t[g] = mm(keys_t[0:512, :], all_rows(probs, g)).astype(BF16)
        return 0

    def out_lower(g, _):
        out_t[g] = mm(keys_t[0:512, 0:1024], low_rows(probs, g)).astype(BF16)
        return 0

    lax.fori_loop(0, 2, out_high, 0)
    lax.fori_loop(2, 4, out_lower, 0)

    def by_head(ref, pair_of_heads):
        lanes = pl.ds(pl.multiple_of(pair_of_heads * 128, 128), 128)
        parts = [ref[g, 0:512, lanes] for g in (2, 0, 3, 1)]
        return [jnp.concatenate([part[:, k * 64 : k * 64 + 64] for part in parts], axis=1) for k in range(2)]

    def value_terms(pair_of_heads, _):
        for k, left in enumerate(by_head(out_t, pair_of_heads)):
            lanes = pl.ds(pl.multiple_of(pair_of_heads * 256 + k * 128, 128), 128)
            right = jnp.concatenate([gout_o[:, lanes], gout_p[:, lanes]], axis=0)
            up[0, :, :, lanes] = mm(left, right).astype(BF16).reshape(4, 128, 128)
        return 0

    lax.fori_loop(0, 4, value_terms, 0)
    start("C00", "C10")

    def full_high(g, _):
        dq_t[g] = mm(keys_t[0:576, :], all_rows(gscore, g)).astype(BF16)
        return 0

    def full_lower(g, _):
        dq_t[g] = mm(keys_t[0:576, 0:1024], low_rows(gscore, g)).astype(BF16)
        return 0

    lax.fori_loop(0, 2, full_high, 0)
    lax.fori_loop(2, 4, full_lower, 0)
    start("ro1", "ro3")

    def sum_core(i):
        wait(f"C0{i}", f"C1{i}")
        uzs[i] = (up[i, f2].astype(F32) + uc[i, 1].astype(F32)).astype(BF16)
        start(f"Z{i}")

    sum_core(0)

    def key_terms(pair_of_heads, _):
        for k, left in enumerate(by_head(dq_t, pair_of_heads)):
            lanes = pl.ds(pl.multiple_of(pair_of_heads * 256 + k * 128, 128), 128)
            right = jnp.concatenate([nope_o[:, lanes], nope_p[:, lanes]], axis=0)
            up[1, :, :, lanes] = mm(left, right).astype(BF16).reshape(4, 128, 128)
            back = mm(wk_t[lanes, :], left)
            gn_own[lanes, :] = back[:, 0:128]
            gn_send[lanes, :] = back[:, 128:256].astype(BF16)
        return 0

    lax.fori_loop(0, 4, key_terms, 0)
    start("C01", "C11", "gn")

    def sum_far(i):
        wait(f"Z{i}")
        whole = up[i, f].astype(F32) + uc[i, 0].astype(F32) + uz[i].astype(F32)
        us1[i] = whole.astype(BF16).reshape(4, 2, 16, 1024)
        start(f"P{i}")

    def sum_pair(i):
        wait(f"P{i}")
        us2[i] = (us1[i, :, zl].astype(F32) + upr[i].astype(F32)).astype(BF16)
        start(f"Yp{i}", f"Ym{i}", f"Y2{i}")

    def sum_y(i):
        wait(f"Yp{i}", f"Ym{i}", f"Y2{i}")
        whole = us2[i, y].astype(F32) + uyr[i, 0].astype(F32) + uyr[i, 1].astype(F32) + uyr[i, 2].astype(F32)
        us3[i] = whole.astype(BF16)
        start(f"Xp{i}", f"Xm{i}", f"X2{i}")

    def sum_x(i, lanes):
        wait(f"Xp{i}", f"Xm{i}", f"X2{i}")
        whole = us3[i].astype(F32) + uxr[i, 0].astype(F32) + uxr[i, 1].astype(F32) + uxr[i, 2].astype(F32)
        mine_rows = whole[0:4]
        for xx in range(1, 4):
            mine_rows = jnp.where(x == xx, whole[xx * 4 : xx * 4 + 4], mine_rows)
        gu_out[:, lanes] = mine_rows

    def b_second(i):
        wait(f"B1{i}")
        add_into(dkb.at[turns[i], xp if i % 2 == 0 else xm, pl.ds(80, 64)], rb1.at[i])
        start(f"B2p{i}", f"B2m{i}")

    def b_last(i):
        wait(f"B2p{i}", f"B2m{i}")
        add_into(dkb.at[turns[i], x, pl.ds(80, 64)], rb2.at[i, 0], rb2.at[i, 1])

    def key_turn(i, _):
        t = (y + jnp.where(i == 0, 2, jnp.where(i == 1, 1, jnp.where(i == 2, 3, 0)))) % 4
        low = mm(gscore[t], query[0]) + mm(gscore[4 + t], query[1]) + mm(gscore[8 + t], query[2]) + mm(gscore[12 + t], query[3])
        low_value = mm(probs[t], grad[0]) + mm(probs[4 + t], grad[1]) + mm(probs[8 + t], grad[2]) + mm(probs[12 + t], grad[3])
        dkb[t, :, 0:64] = (low[:, 0:512] + low_value).astype(BF16).reshape(4, 64, 512)
        high = mm(gscore[16 + t], query[0]) + mm(gscore[20 + t], query[1])
        high_value = mm(probs[16 + t], grad[0]) + mm(probs[20 + t], grad[1])
        dkb[t, :, 80:144] = (high[:, 0:512] + high_value).astype(BF16).reshape(4, 64, 512)
        for xx in range(4):
            rows = [half[xx * 64 + s * 16 : xx * 64 + s * 16 + 16, 512:576] for half in (low, high) for s in range(4)]
            dkb[t, xx, 64:80] = jnp.concatenate(rows, axis=1).astype(BF16)

        @pl.when(i == 0)
        def _():
            start("A1p", "A1m", "B10")
            sum_core(1)

        @pl.when(i == 1)
        def _():
            wait("A1p")
            add_into(dkb.at[yp, pl.ds(0, 2), pl.ds(0, 80)], ra1.at[0])
            start("A2p", "B11")
            b_second(0)

        @pl.when(i == 2)
        def _():
            wait("A1m")
            add_into(dkb.at[ym, pl.ds(2, 2), pl.ds(0, 80)], ra1.at[1])
            start("A2m", "B12")
            b_second(1)
            b_last(0)
            start("B3p", "B3m")
            sum_far(0)

        @pl.when(i == 3)
        def _():
            start("B13")
            wait("A2p", "A2m")
            add_into(dkb.at[y, :, pl.ds(0, 80)], ra2.at[0], ra2.at[1])
            start("A3p", "A3m")
            b_second(2)
            b_last(1)
            wait("B3p")
            add_into(dkb.at[yp, x, pl.ds(80, 32)], rb3.at[0])
            start("B4p")
            b_second(3)

        return 0

    lax.fori_loop(0, 4, key_turn, 0)
    sum_pair(0)
    b_last(2)
    wait("B3m")
    add_into(dkb.at[ym, x, pl.ds(112, 32)], rb3.at[1])
    start("B4m")
    wait("A3p")
    add_into(dkb.at[y, xp, pl.ds(0, 48)], ra3.at[pl.ds(0, 48)])
    start("A4p")
    wait("A3m")
    add_into(dkb.at[y, xm, pl.ds(48, 32)], ra3.at[pl.ds(48, 32)])
    start("A4m")
    sum_far(1)
    sum_y(0)

    wait("gn", "ro1", "ro3")
    gn_out[...] = jnp.transpose(gn_own[...] + gn_recv[...].astype(F32)).astype(BF16)
    for half, g, slot in ((0, 2, 1), (1, 0, 0)):
        rope = dq_t[g, 512:576].astype(F32) + ro_recv[slot].astype(F32)
        rope = jnp.transpose(rope)
        gr_out[half * 64 : half * 64 + 64, :] = jnp.concatenate(
            [rope[h * 64 : h * 64 + 64] for h in range(HEADS)], axis=1
        ).astype(BF16)

    sum_pair(1)
    b_last(3)
    wait("A4p", "A4m")
    upper = dkb[y, x, 0:80].astype(F32) + ra4[0].astype(F32) + ra4[1].astype(F32)
    gl_out[0:64, 0:512] = upper[0:64].astype(BF16)
    for s in range(8):
        gl_out[s * 16 : s * 16 + 16, 512:576] = upper[64:80, s * 64 : s * 64 + 64].astype(BF16)
    wait("B4p", "B4m")
    lower = dkb[y, x, 80:144].astype(F32) + rb4[0].astype(F32) + rb4[1].astype(F32)
    gl_out[64:128, 0:512] = lower.astype(BF16)
    sum_y(1)
    sum_x(0, slice(1024, 2048))
    sum_x(1, slice(0, 1024))
    for name in made:
        made[name]().wait_send()


def per_device(query_nope, query_rope, latent, grad_out, w_up, block_order):
    shapes = [
        ((16, 144, 512), BF16), ((8, 256, 640), BF16), ((640, 2048), BF16),
        ((128, 1024), BF16), ((128, 512), BF16), ((128, 1024), BF16), ((4, 128, 2048), BF16), ((1024, 512), BF16),
        ((4, 512, 640), BF16), ((4, 512, 512), BF16), ((24, 256, 512), BF16), ((24, 256, 512), F32), ((24, 256, 512), BF16),
        ((24, 1, 512), F32), ((4, 1, 512), F32), ((4, 1, 512), F32), ((4, 1, 512), F32), ((4, 8, 512), F32), ((4, 8, 512), F32),
        ((4, 576, 512), BF16), ((4, 512, 512), BF16), ((1024, 128), F32), ((1024, 128), BF16), ((1024, 128), BF16), ((2, 64, 512), BF16),
        ((4, 4, 144, 512), BF16), ((2, 2, 80, 512), BF16), ((2, 4, 80, 512), BF16), ((80, 512), BF16), ((2, 80, 512), BF16),
        ((4, 64, 512), BF16), ((4, 2, 64, 512), BF16), ((2, 32, 512), BF16), ((2, 64, 512), BF16),
        ((2, 4, 128, 1024), BF16), ((2, 2, 128, 1024), BF16), ((2, 128, 1024), BF16), ((2, 128, 1024), BF16),
        ((2, 4, 2, 16, 1024), BF16), ((2, 4, 16, 1024), BF16), ((2, 4, 16, 1024), BF16), ((2, 3, 16, 1024), BF16),
        ((2, 16, 1024), BF16), ((2, 3, 16, 1024), BF16),
    ]
    vmem = pl.BlockSpec(memory_space=pltpu.VMEM)
    gn, gr, gl, gu = pl.pallas_call(
        kernel,
        out_shape=(
            jax.ShapeDtypeStruct((128, 1024), BF16),
            jax.ShapeDtypeStruct((128, 512), BF16),
            jax.ShapeDtypeStruct((128, 576), BF16),
            jax.ShapeDtypeStruct((4, 2048), F32),
        ),
        in_specs=[pl.BlockSpec(memory_space=pltpu.SMEM)] + [vmem] * 5,
        out_specs=(vmem,) * 4,
        scratch_shapes=[pltpu.VMEM(shape, dtype) for shape, dtype in shapes]
        + [pltpu.SemaphoreType.DMA((COPIES,)), pltpu.SemaphoreType.DMA((COPIES,))],
        compiler_params=pltpu.CompilerParams(
            collective_id=0, has_side_effects=True, vmem_limit_bytes=63 * 1024 * 1024
        ),
        name="latent_attention_backward",
    )(block_order, latent[0], query_nope[0], query_rope[0], grad_out[0], w_up)
    return gn[None], gr[None], gl[None], gu


def solution(mesh):
    rows = P("fsdp", "blk", None)
    return jax.shard_map(
        per_device,
        mesh=mesh,
        in_specs=(rows, rows, rows, rows, P("fsdp", None), P()),
        out_specs=(rows, rows, rows, P(("fsdp", "blk"), None)),
        check_vma=False,
    )
```

```python
import functools
import math

import jax
import jax.numpy as jnp
from jax import lax
from jax.experimental import pallas as pl
from jax.experimental.pallas import tpu as pltpu
from jax.sharding import PartitionSpec as P

HEADS = 8
LATENT = 512
SCALE = 1.0 / math.sqrt(192.0)
NEG_FILL = -1e30
F32 = jnp.float32
BF16 = jnp.bfloat16
MESH = pl.DeviceIdType.MESH
COPIES = 112


def mm(a, b):
    return lax.dot_general(a, b, (((1,), (0,)), ((), ())), preferred_element_type=F32)


def mm_nt(a, b):
    return lax.dot_general(a, b, (((1,), (1,)), ((), ())), preferred_element_type=F32)


def add_into(ref, *others):
    total = ref[...].astype(F32)
    for other in others:
        total = total + other[...].astype(F32)
    ref[...] = total.astype(BF16)


def kernel(
    order, lat, nope_o, rope_o, gout_o, w_own,
    gn_out, gr_out, gl_out, gu_out,
    kbuf, keys, keys_t, nope_p, rope_p, gout_p, w_all, wk_t,
    query, grad, probs, gprob, gscore, peaks, peak, total, centre, stat_s, stat_r,
    dq_t, out_t, gn_own, gn_send, gn_recv, ro_recv,
    dkb, ra1, ra2, ra3, rb1, rb2, rb3,
    up, uc, uzs, uz, us2, uyr, us3, uxr,
    send, recv,
):
    f = lax.axis_index("fsdp")
    blk = lax.axis_index("blk")
    x, zl, y = blk % 4, (blk // 4) % 2, blk // 8
    xp, xm, x2 = (x + 1) % 4, (x + 3) % 4, (x + 2) % 4
    yp, ym, y2 = (y + 1) % 4, (y + 3) % 4, (y + 2) % 4
    f1 = f + 1 - 2 * (f % 2)
    f2 = (f + 2) % 4
    f3 = (f1 + 2) % 4
    pair_blk = blk + 4 - 8 * zl

    def at(yy, xx):
        return {"blk": (yy * 2 + zl) * 4 + xx}

    to_xp, to_xm, to_x2 = at(y, xp), at(y, xm), at(y, x2)
    to_yp, to_ym, to_y2 = at(yp, x), at(ym, x), at(y2, x)
    to_pair = {"blk": pair_blk}
    to_core = {"fsdp": f1}
    to_far = {"fsdp": f2, "blk": pair_blk}
    to_z2 = {"fsdp": f2}

    made = {}

    def define(name, src, dst, device):
        number = len(made)
        made[name] = lambda: pltpu.make_async_remote_copy(
            src_ref=src(), dst_ref=dst(), send_sem=send.at[number], recv_sem=recv.at[number],
            device_id=device, device_id_type=MESH,
        )

    def start(*names):
        for name in names:
            made[name]().start()

    def wait(*names):
        for name in names:
            made[name]().wait_recv()

    def same(name, part, device):
        define(name, part, part, device)

    for name, first, swap in (("a", 0, False), ("b", 288, True)):
        def part(dy, dx, first=first, swap=swap):
            if swap:
                dy, dx = dx, dy
            return lambda: kbuf.at[((y + dy) % 4) * 4 + (x + dx) % 4, pl.ds(first, 288)]

        if swap:
            ip, im, i2, jp, jm = to_yp, to_ym, to_y2, to_xp, to_xm
        else:
            ip, im, i2, jp, jm = to_xp, to_xm, to_x2, to_yp, to_ym
        same(name + "1", part(0, 0), ip)
        same(name + "2", part(0, 0), im)
        same(name + "5", part(0, 0), i2)
        same(name + "3", part(0, 0), jp)
        same(name + "4", part(0, 0), jm)
        same(name + "7", part(0, 3), jp)
        same(name + "8", part(0, 3), jm)
        same(name + "9", part(0, 1), jp)
        same(name + "10", part(0, 1), jm)
        same(name + "11", part(0, 2), jp)
        same(name + "12", part(0, 2), jm)
        same(name + "13", part(3, 0), jp)
        same(name + "14", part(3, 3), jp)
        same(name + "15", part(1, 1), jm)
        same(name + "16", part(1, 2), jm)

    define("qn", lambda: nope_o, lambda: nope_p, to_pair)
    define("qr", lambda: rope_o, lambda: rope_p, to_pair)
    define("qg", lambda: gout_o, lambda: gout_p, to_pair)
    for name, first in (("k", 0), ("v", 1024)):
        def own_w(first=first):
            return w_own.at[:, pl.ds(first, 1024)]

        def far_w(shard, first=first):
            return lambda: w_all.at[shard, :, pl.ds(first, 1024)]

        define(f"w{name}1", own_w, far_w(f), to_core)
        define(f"w{name}2", own_w, far_w(f), to_far)
        define(f"w{name}3", far_w(f2), far_w(f2), to_core)
    define("st0", lambda: stat_s.at[pl.ds(0, 2)], lambda: stat_r.at[pl.ds(2, 2)], to_pair)
    define("st1", lambda: stat_s.at[pl.ds(2, 2)], lambda: stat_r.at[pl.ds(0, 2)], to_pair)
    define("gn", lambda: gn_send, lambda: gn_recv, to_pair)
    define("ro0", lambda: dq_t.at[2, pl.ds(512, 64)], lambda: ro_recv.at[0], to_pair)
    define("ro1", lambda: dq_t.at[3, pl.ds(512, 64)], lambda: ro_recv.at[1], to_pair)

    def term(yy, xx, first):
        return lambda: dkb.at[yy, xx, pl.ds(first, 288)]

    def term_rows(yy, x_first, x_count):
        return lambda: dkb.at[yy, pl.ds(x_first, x_count), pl.ds(0, 288)]

    define("A1p", term_rows(y2, 0, 2), lambda: ra1.at[0], to_yp)
    define("A1m", term_rows(y2, 2, 2), lambda: ra1.at[1], to_ym)
    define("A2p", term_rows(yp, 0, 4), lambda: ra2.at[0], to_yp)
    define("A2m", term_rows(ym, 0, 4), lambda: ra2.at[1], to_ym)
    define("A3p", term(y, xp, 0), lambda: ra3.at[0], to_xp)
    define("A3m", term(y, xm, 0), lambda: ra3.at[1], to_xm)
    define("A32", term(y, x2, 0), lambda: ra3.at[2], to_x2)
    turns = (y2, yp, ym, y)
    for i in range(4):
        to_first = to_x2 if i == 3 else (to_xp if i % 2 == 0 else to_xm)
        define(f"B1{i}", term(turns[i], x2, 288), lambda i=i: rb1.at[i], to_first)
        define(f"B2p{i}", term(turns[i], xp, 288), lambda i=i: rb2.at[i, 0], to_xp)
        define(f"B2m{i}", term(turns[i], xm, 288), lambda i=i: rb2.at[i, 1], to_xm)
    for i, device in enumerate((to_y2, to_yp, to_ym)):
        define(f"B3{i}", term(turns[i], x, 288), lambda i=i: rb3.at[i], device)

    for i in range(2):
        define(f"C0{i}", lambda i=i: up.at[i, f1], lambda i=i: uc.at[i, 0], to_core)
        define(f"C1{i}", lambda i=i: up.at[i, f3], lambda i=i: uc.at[i, 1], to_core)
        for j, device in enumerate((to_pair, to_far, to_z2)):
            define(f"Z{j}{i}", lambda i=i, j=j: uzs.at[i, j], lambda i=i, j=j: uz.at[i, j], device)
        for j, (yy, device) in enumerate(((yp, to_yp), (ym, to_ym), (y2, to_y2))):
            define(f"Y{j}{i}", lambda i=i, yy=yy: us2.at[i, yy], lambda i=i, j=j: uyr.at[i, j], device)
        for j, device in enumerate((to_xp, to_xm, to_x2)):
            define(f"X{j}{i}", lambda i=i: us3.at[i], lambda i=i, j=j: uxr.at[i, j], device)

    kbuf[y * 4 + x] = lat[...]
    barrier = pltpu.get_barrier_semaphore()
    partners = (to_xp, to_xm, to_x2, to_yp, to_ym, to_y2, to_pair, to_core, to_far, to_z2)
    for partner in partners:
        pl.semaphore_signal(barrier, inc=1, device_id=partner, device_id_type=MESH)
    pl.semaphore_wait(barrier, len(partners))

    start("wk2", "qn", "a1", "b1", "a2", "b2", "a5", "b5", "a3", "b3", "a4", "b4", "qr", "wk1")
    w_all[f] = w_own[...]
    query[:, 512:640, :] = jnp.zeros((4, 128, 512), BF16)
    keys[:, :, 512:640] = jnp.zeros((8, 256, 128), BF16)

    def place_rope(rope, s):
        for k in range(4):
            turned = jnp.transpose(rope[:, k * 128 : k * 128 + 128].astype(F32))
            lanes = slice(k * 128, k * 128 + 128)
            query[2 * s + 1, 512:576, lanes] = jnp.concatenate([turned[:64, :64], turned[64:, :64]], axis=1).astype(BF16)
            query[2 * s, 512:576, lanes] = jnp.concatenate([turned[:64, 64:], turned[64:, 64:]], axis=1).astype(BF16)

    place_rope(rope_o, 0)
    for name in ("a", "b"):
        wait(name + "1")
        start(name + "7", name + "8")
    for name in ("a", "b"):
        wait(name + "2")
        start(name + "9", name + "10")
    for name in ("a", "b"):
        wait(name + "5")
        start(name + "11", name + "12")
    start("wv2", "qg", "wv1")
    for name in ("a", "b"):
        wait(name + "3")
        start(name + "13")
    wait("wk2")
    start("wk3")
    for name in ("a", "b"):
        wait(name + "7")
        start(name + "14")
    for name in ("a", "b"):
        wait(name + "10")
        start(name + "15")
    for name in ("a", "b"):
        wait(name + "12")
        start(name + "16")

    def blocks(value, lanes):
        both = value[:, lanes]
        empty = jnp.zeros((64, 128), BF16)
        rows = []
        for half in (both[:64], both[64:]):
            rows.append(jnp.concatenate([half[:, :128], empty], axis=1))
            rows.append(jnp.concatenate([empty, half[:, 128:]], axis=1))
        return jnp.concatenate(rows, axis=0)

    def project(value, first, ref, s):
        def two_heads(k, _):
            lanes = pl.ds(pl.multiple_of(k * 256, 256), 256)
            w_lanes = pl.ds(pl.multiple_of(first + k * 256, 256), 256)
            to = pl.ds(pl.multiple_of(k * 128, 128), 128)
            out = mm_nt(w_all[:, :, w_lanes].reshape(512, 256), blocks(value, lanes)).astype(BF16)
            ref[2 * s + 1, 0:512, to] = out[:, :128]
            ref[2 * s, 0:512, to] = out[:, 128:]
            return 0

        lax.fori_loop(0, 4, two_heads, 0)

    wait("wk1", "wk3")
    project(nope_o, 0, query, 0)
    for s in range(4):
        wk_t[:, s * 128 : s * 128 + 128] = jnp.transpose(w_all[s, :, 0:1024])
    wait("qn", "qr")
    place_rope(rope_p, 1)
    project(nope_p, 0, query, 1)

    for name in ("a", "b"):
        wait(*(name + n for n in ("4", "8", "9", "11", "13", "14", "15", "16")))

    def assemble(i, _):
        yy, xx = i // 2, (i % 2) * 2
        both = [kbuf[yy * 4 + xx + j] for j in range(2)]
        lanes = pl.ds(pl.multiple_of(i * 128, 128), 128)
        high_lanes = pl.ds(pl.multiple_of(1024 + i * 128, 128), 128)
        keys_t[:, lanes] = jnp.concatenate([b[:, :64] for b in both], axis=1)
        keys_t[:, high_lanes] = jnp.concatenate([b[:, 64:] for b in both], axis=1)
        for j in range(2):
            rows = pl.ds(pl.multiple_of((xx + j) * 64, 64), 64)
            main = jnp.transpose(both[j][:512])
            rest = jnp.transpose(both[j][512:])
            keys[yy, rows, 0:512] = main[:64]
            keys[yy, rows, 512:576] = rest[:64]
            keys[4 + yy, rows, 0:512] = main[64:]
            keys[4 + yy, rows, 512:576] = rest[64:]
        return 0

    lax.fori_loop(0, 8, assemble, 0)
    wait("wv2")
    start("wv3")
    wait("wv1", "wv3")
    project(gout_o, 1024, grad, 0)

    peak[...] = jnp.full((4, 1, 512), NEG_FILL, F32)
    total[...] = jnp.zeros((4, 1, 512), F32)
    centre[...] = jnp.zeros((4, 1, 512), F32)
    relative = lax.broadcasted_iota(jnp.int32, (64, 512), 0) - lax.broadcasted_iota(jnp.int32, (64, 512), 1) % 64

    def visit(t, g, high, masked, first):
        tile = 4 + t if high else t
        slot = 16 + (g // 2) * 4 + t if high else g * 4 + t
        scores = mm(keys[tile], query[g])
        grad_probs = mm(keys[tile, :, 0:512], grad[g])
        if masked:
            block = 63 - first if high else first
            parts = []
            for xx in range(4):
                key_first = order[0, (t * 2 + zl) * 4 + xx]
                key_block = 63 - key_first if high else key_first
                parts.append(relative <= (block - key_block) * 64)
            allowed = jnp.concatenate(parts, axis=0)
            scores = jnp.where(allowed, scores, NEG_FILL)
        old = peak[g]
        new = jnp.maximum(old, jnp.max(scores, axis=0, keepdims=True))
        weights = jnp.exp((scores - new) * SCALE)
        if masked:
            weights = jnp.where(allowed, weights, 0.0)
        factor = jnp.exp((old - new) * SCALE)
        total[g] = total[g] * factor + jnp.sum(weights, axis=0, keepdims=True)
        centre[g] = centre[g] * factor + jnp.sum(weights * grad_probs, axis=0, keepdims=True)
        peak[g] = new
        probs[slot] = weights.astype(BF16)
        gprob[slot] = grad_probs
        peaks[slot] = new

    def visits(s, first):
        def step(t, _):
            visit(t, 2 * s, False, False, first)
            visit(t, 2 * s + 1, False, True, first)
            visit(t, 2 * s, True, True, first)
            return 0

        lax.fori_loop(0, 4, step, 0)
        for g in (2 * s, 2 * s + 1):
            stat_s[g, 0:1] = peak[g]
            stat_s[g, 1:2] = total[g]
            stat_s[g, 2:3] = centre[g]
        start(f"st{s}")

    visits(0, order[0, blk])
    wait("qg")
    project(gout_p, 1024, grad, 1)
    visits(1, order[0, pair_blk])

    def normalise(slot, g):
        factor = jnp.exp((peaks[slot] - peak[g]) * SCALE) / total[g]
        p = probs[slot].astype(F32) * factor
        probs[slot] = p.astype(BF16)
        gscore[slot] = (p * (gprob[slot] - centre[g]) * SCALE).astype(BF16)

    def low_rows(ref, g):
        return ref[g * 4 : g * 4 + 4].reshape(1024, 512)

    def all_rows(ref, g):
        return jnp.concatenate([low_rows(ref, g), ref[16 + g * 2 : 20 + g * 2].reshape(1024, 512)], axis=0)

    def merge(s):
        wait(f"st{1 - s}")
        for g in (2 * s, 2 * s + 1):
            here, there = stat_s[g], stat_r[g]
            new = jnp.maximum(here[0:1], there[0:1])
            f_here = jnp.exp((here[0:1] - new) * SCALE)
            f_there = jnp.exp((there[0:1] - new) * SCALE)
            norm = here[1:2] * f_here + there[1:2] * f_there
            peak[g] = new
            total[g] = norm
            centre[g] = (here[2:3] * f_here + there[2:3] * f_there) / norm

        def low_slots(i, _):
            normalise(s * 8 + i, 2 * s + i // 4)
            return 0

        def high_slots(i, _):
            normalise(16 + s * 4 + i, 2 * s)
            return 0

        lax.fori_loop(0, 8, low_slots, 0)
        lax.fori_loop(0, 4, high_slots, 0)
        out_t[2 * s] = mm(keys_t[0:512, :], all_rows(probs, 2 * s)).astype(BF16)
        out_t[2 * s + 1] = mm(keys_t[0:512, 0:1024], low_rows(probs, 2 * s + 1)).astype(BF16)

    merge(1)
    merge(0)

    def two_heads_of(ref, k):
        lanes = pl.ds(pl.multiple_of(k * 128, 128), 128)
        return jnp.concatenate([ref[g, 0:512, lanes] for g in range(4)], axis=1)

    def two_heads_rows(own, pair, k):
        lanes = pl.ds(pl.multiple_of(k * 256, 256), 256)
        mine, other = blocks(own, lanes), blocks(pair, lanes)
        return jnp.concatenate([mine[128:], mine[:128], other[128:], other[:128]], axis=0)

    def value_terms(k, _):
        lanes = pl.ds(pl.multiple_of(k * 256, 256), 256)
        whole = mm(two_heads_of(out_t, k), two_heads_rows(gout_o, gout_p, k))
        up[0, :, :, lanes] = whole.astype(BF16).reshape(4, 128, 256)
        return 0

    lax.fori_loop(0, 4, value_terms, 0)
    start("C00", "C10")

    for s in (1, 0):
        dq_t[2 * s] = mm(keys_t[...], all_rows(gscore, 2 * s)).astype(BF16)
        dq_t[2 * s + 1] = mm(keys_t[:, 0:1024], low_rows(gscore, 2 * s + 1)).astype(BF16)

    def sum_core(i):
        wait(f"C0{i}", f"C1{i}")
        for j, (shard, slot, plane) in enumerate(((f, 0, 1 - zl), (f2, 1, 1 - zl), (f2, 1, zl))):
            for yy in range(4):
                rows = pl.ds(pl.multiple_of(yy * 32 + plane * 16, 16), 16)
                whole = up[i, shard, rows].astype(F32) + uc[i, slot, rows].astype(F32)
                uzs[i, j, yy] = whole.astype(BF16)
        start(f"Z0{i}", f"Z1{i}", f"Z2{i}")

    sum_core(0)

    def key_terms(k, _):
        lanes = pl.ds(pl.multiple_of(k * 256, 256), 256)
        left = two_heads_of(dq_t, k)
        whole = mm(left, two_heads_rows(nope_o, nope_p, k))
        up[1, :, :, lanes] = whole.astype(BF16).reshape(4, 128, 256)
        back = mm(wk_t[lanes, :], left)
        for j in range(2):
            rows = pl.ds(pl.multiple_of(k * 256 + j * 128, 128), 128)
            tiles = [back[j * 128 : j * 128 + 128, g * 128 + j * 64 : g * 128 + j * 64 + 64] for g in range(4)]
            gn_own[rows, :] = jnp.concatenate([tiles[1], tiles[0]], axis=1)
            gn_send[rows, :] = jnp.concatenate([tiles[3], tiles[2]], axis=1).astype(BF16)
        return 0

    lax.fori_loop(0, 4, key_terms, 0)
    start("C01", "C11")

    def sum_z(i):
        wait(f"Z0{i}", f"Z1{i}", f"Z2{i}")
        for yy in range(4):
            rows = pl.ds(pl.multiple_of(yy * 32 + zl * 16, 16), 16)
            whole = up[i, f, rows].astype(F32) + uc[i, 0, rows].astype(F32)
            for j in range(3):
                whole = whole + uz[i, j, yy].astype(F32)
            us2[i, yy] = whole.astype(BF16)
        start(f"Y0{i}", f"Y1{i}", f"Y2{i}")

    def sum_y(i):
        wait(f"Y0{i}", f"Y1{i}", f"Y2{i}")
        whole = us2[i, y].astype(F32) + uyr[i, 0].astype(F32) + uyr[i, 1].astype(F32) + uyr[i, 2].astype(F32)
        us3[i] = whole.astype(BF16)
        start(f"X0{i}", f"X1{i}", f"X2{i}")

    def sum_x(i, lanes):
        wait(f"X0{i}", f"X1{i}", f"X2{i}")
        whole = us3[i].astype(F32) + uxr[i, 0].astype(F32) + uxr[i, 1].astype(F32) + uxr[i, 2].astype(F32)
        mine_rows = whole[0:4]
        for xx in range(1, 4):
            mine_rows = jnp.where(x == xx, whole[xx * 4 : xx * 4 + 4], mine_rows)
        gu_out[:, lanes] = mine_rows

    lower = pl.ds(288, 288)

    def b_second(i):
        wait(f"B1{i}")
        add_into(dkb.at[turns[i], xp if i % 2 == 0 else xm, lower], rb1.at[i])
        start(f"B2p{i}", f"B2m{i}")

    def b_last(i):
        wait(f"B2p{i}", f"B2m{i}")
        add_into(dkb.at[turns[i], x, lower], rb2.at[i, 0], rb2.at[i, 1])
        start(f"B3{i}")

    def key_turn(i, _):
        t = (y + jnp.where(i == 0, 2, jnp.where(i == 1, 1, jnp.where(i == 2, 3, 0)))) % 4

        def one(slots):
            a = sum(mm_nt(query[g, 0:576], gscore[slot]) for g, slot in slots)
            b = sum(mm_nt(grad[g], probs[slot]) for g, slot in slots)
            return a[:512] + b, a[512:]

        low, low_rest = one([(g, g * 4 + t) for g in range(4)])
        high, high_rest = one([(2 * s, 16 + s * 4 + t) for s in range(2)])
        for xx in range(4):
            lanes = slice(xx * 64, xx * 64 + 64)
            dkb[t, xx, 0:512] = jnp.concatenate([low[:, lanes], high[:, lanes]], axis=1).astype(BF16)
            dkb[t, xx, 512:576] = jnp.concatenate([low_rest[:, lanes], high_rest[:, lanes]], axis=1).astype(BF16)

        @pl.when(i == 0)
        def _():
            start("A1p", "A1m", "B10")
            sum_core(1)
            start("ro0", "ro1", "gn")

        @pl.when(i == 1)
        def _():
            start("B11")
            wait("A1p")
            add_into(dkb.at[yp, pl.ds(0, 2), pl.ds(0, 288)], ra1.at[0])
            start("A2p")
            b_second(0)

        @pl.when(i == 2)
        def _():
            start("B12")
            wait("A1m")
            add_into(dkb.at[ym, pl.ds(2, 2), pl.ds(0, 288)], ra1.at[1])
            start("A2m")
            b_second(1)
            b_last(0)
            sum_z(0)

        @pl.when(i == 3)
        def _():
            start("B13", "B2p3", "B2m3")
            wait("A2p", "A2m")
            add_into(dkb.at[y, :, pl.ds(0, 288)], ra2.at[0], ra2.at[1])
            start("A3p", "A3m", "A32")
            b_second(2)
            b_last(1)
            sum_z(1)
            sum_y(0)

        return 0

    lax.fori_loop(0, 4, key_turn, 0)
    b_last(2)
    sum_y(1)

    wait("gn", "ro0", "ro1")
    gn_out[...] = jnp.transpose(gn_own[...] + gn_recv[...].astype(F32)).astype(BF16)
    for half, g in ((0, 1), (1, 0)):
        rope = jnp.transpose(dq_t[g, 512:576].astype(F32) + ro_recv[g].astype(F32))
        gr_out[half * 64 : half * 64 + 64, :] = jnp.concatenate(
            [rope[h * 64 : h * 64 + 64] for h in range(HEADS)], axis=1
        ).astype(BF16)

    wait("A3p", "A3m", "A32")
    add_into(dkb.at[y, x, pl.ds(0, 288)], ra3.at[0], ra3.at[1], ra3.at[2])
    wait("B13", "B2p3", "B2m3", "B30", "B31", "B32")
    add_into(dkb.at[y, x, lower], rb1.at[3], rb2.at[3, 0], rb2.at[3, 1], rb3.at[0], rb3.at[1], rb3.at[2])
    gl_out[...] = dkb[y, x]
    sum_x(0, slice(1024, 2048))
    sum_x(1, slice(0, 1024))
    for name in made:
        made[name]().wait_send()


def per_device(query_nope, query_rope, latent, grad_out, w_up, block_order):
    shapes = [
        ((16, 576, 128), BF16), ((8, 256, 640), BF16), ((576, 2048), BF16),
        ((128, 1024), BF16), ((128, 512), BF16), ((128, 1024), BF16), ((4, 128, 2048), BF16), ((1024, 512), BF16),
        ((4, 640, 512), BF16), ((4, 512, 512), BF16), ((24, 256, 512), BF16), ((24, 256, 512), F32), ((24, 256, 512), BF16),
        ((24, 1, 512), F32), ((4, 1, 512), F32), ((4, 1, 512), F32), ((4, 1, 512), F32), ((4, 8, 512), F32), ((4, 8, 512), F32),
        ((4, 576, 512), BF16), ((4, 512, 512), BF16), ((1024, 128), F32), ((1024, 128), BF16), ((1024, 128), BF16), ((2, 64, 512), BF16),
        ((4, 4, 576, 128), BF16), ((2, 2, 288, 128), BF16), ((2, 4, 288, 128), BF16), ((3, 288, 128), BF16),
        ((4, 288, 128), BF16), ((4, 2, 288, 128), BF16), ((3, 288, 128), BF16),
        ((2, 4, 128, 1024), BF16), ((2, 2, 128, 1024), BF16), ((2, 3, 4, 16, 1024), BF16), ((2, 3, 4, 16, 1024), BF16),
        ((2, 4, 16, 1024), BF16), ((2, 3, 16, 1024), BF16), ((2, 16, 1024), BF16), ((2, 3, 16, 1024), BF16),
    ]
    vmem = pl.BlockSpec(memory_space=pltpu.VMEM)
    gn, gr, gl, gu = pl.pallas_call(
        kernel,
        out_shape=(
            jax.ShapeDtypeStruct((128, 1024), BF16),
            jax.ShapeDtypeStruct((128, 512), BF16),
            jax.ShapeDtypeStruct((576, 128), BF16),
            jax.ShapeDtypeStruct((4, 2048), F32),
        ),
        in_specs=[pl.BlockSpec(memory_space=pltpu.SMEM)] + [vmem] * 5,
        out_specs=(vmem,) * 4,
        scratch_shapes=[pltpu.VMEM(shape, dtype) for shape, dtype in shapes]
        + [pltpu.SemaphoreType.DMA((COPIES,)), pltpu.SemaphoreType.DMA((COPIES,))],
        compiler_params=pltpu.CompilerParams(
            collective_id=0, has_side_effects=True, vmem_limit_bytes=63 * 1024 * 1024
        ),
        name="latent_attention_backward",
    )(block_order.T, latent[0].T, query_nope[0], query_rope[0], grad_out[0], w_up)
    return gn[None], gr[None], gl.T[None], gu


def solution(mesh):
    rows = P("fsdp", "blk", None)
    return jax.shard_map(
        per_device,
        mesh=mesh,
        in_specs=(rows, rows, rows, rows, P("fsdp", None), P()),
        out_specs=(rows, rows, rows, P(("fsdp", "blk"), None)),
        check_vma=False,
    )
```

```python
import functools
import math

import jax
import jax.numpy as jnp
from jax import lax
from jax.experimental import pallas as pl
from jax.experimental.pallas import tpu as pltpu
from jax.sharding import PartitionSpec as P

HEADS = 8
LATENT = 512
SCALE = 1.0 / math.sqrt(192.0)
NEG_FILL = -1e30
NEG_START = -1e20
BASE2 = SCALE * math.log2(math.e)
F32 = jnp.float32
BF16 = jnp.bfloat16
MESH = pl.DeviceIdType.MESH
COPIES = 144


def mm(a, b):
    return lax.dot_general(a, b, (((1,), (0,)), ((), ())), preferred_element_type=F32)


def mm_nt(a, b):
    return lax.dot_general(a, b, (((1,), (1,)), ((), ())), preferred_element_type=F32)


def add_into(ref, *others):
    total = ref[...].astype(F32)
    for other in others:
        total = total + other[...].astype(F32)
    ref[...] = total.astype(BF16)


def kernel(
    order, lat_in, nope_in, rope_in, gout_in, w_in,
    gn_out, gr_out, gl_out, gu_out,
    kbuf, keys, keys_t, nope_p, rope_p, gout_p, w_all, wk_t,
    query, grad, probs, gprob, gscore, peaks, peak, total, centre, stat_s, stat_r,
    dq_t, out_t, gn_own, gn_send, gn_recv, ro_recv,
    dkb, ra1, ra2, ra3, rb1, rb2, rb3,
    up, uc, uzs, uz, us2, uyr, us3, uxr,
    lat, nope_o, rope_o, gout_o, w_own, loads,
    send, recv,
):
    f = lax.axis_index("fsdp")
    blk = lax.axis_index("blk")
    x, zl, y = blk % 4, (blk // 4) % 2, blk // 8
    xp, xm, x2 = (x + 1) % 4, (x + 3) % 4, (x + 2) % 4
    yp, ym, y2 = (y + 1) % 4, (y + 3) % 4, (y + 2) % 4
    f1 = f + 1 - 2 * (f % 2)
    f2 = (f + 2) % 4
    f3 = (f1 + 2) % 4
    pair_blk = blk + 4 - 8 * zl

    def at(yy, xx):
        return {"blk": (yy * 2 + zl) * 4 + xx}

    to_xp, to_xm, to_x2 = at(y, xp), at(y, xm), at(y, x2)
    to_yp, to_ym, to_y2 = at(yp, x), at(ym, x), at(y2, x)
    to_pair = {"blk": pair_blk}
    to_core = {"fsdp": f1}
    to_far = {"fsdp": f2, "blk": pair_blk}
    to_z2 = {"fsdp": f2}

    made = {}

    def define(name, src, dst, device):
        number = len(made)
        made[name] = lambda: pltpu.make_async_remote_copy(
            src_ref=src(), dst_ref=dst(), send_sem=send.at[number], recv_sem=recv.at[number],
            device_id=device, device_id_type=MESH,
        )

    def start(*names):
        for name in names:
            made[name]().start()

    def wait(*names):
        for name in names:
            made[name]().wait_recv()

    def same(name, part, device):
        define(name, part, part, device)

    for name, first, swap in (("a", 0, False), ("b", 288, True)):
        def part(dy, dx, first=first, swap=swap):
            if swap:
                dy, dx = dx, dy
            return lambda: kbuf.at[((y + dy) % 4) * 4 + (x + dx) % 4, pl.ds(first, 288)]

        if swap:
            ip, im, i2, jp, jm = to_yp, to_ym, to_y2, to_xp, to_xm
        else:
            ip, im, i2, jp, jm = to_xp, to_xm, to_x2, to_yp, to_ym
        same(name + "1", part(0, 0), ip)
        same(name + "2", part(0, 0), im)
        same(name + "5", part(0, 0), i2)
        same(name + "3", part(0, 0), jp)
        same(name + "4", part(0, 0), jm)
        same(name + "7", part(0, 3), jp)
        same(name + "8", part(0, 3), jm)
        same(name + "9", part(0, 1), jp)
        same(name + "10", part(0, 1), jm)
        same(name + "11", part(0, 2), jp)
        same(name + "12", part(0, 2), jm)
        same(name + "13", part(3, 0), jp)
        same(name + "14", part(3, 3), jp)
        same(name + "15", part(1, 1), jm)
        same(name + "16", part(1, 2), jm)

    define("qn", lambda: nope_o, lambda: nope_p, to_pair)
    define("qr", lambda: rope_o, lambda: rope_p, to_pair)
    define("qg", lambda: gout_o, lambda: gout_p, to_pair)
    for name, first in (("k", 0), ("v", 1024)):
        def own_w(first=first):
            return w_own.at[:, pl.ds(first, 1024)]

        def far_w(shard, first=first):
            return lambda: w_all.at[shard, :, pl.ds(first, 1024)]

        define(f"w{name}1", own_w, far_w(f), to_core)
        define(f"w{name}2", own_w, far_w(f), to_far)
        define(f"w{name}3", far_w(f2), far_w(f2), to_core)
    define("st0", lambda: stat_s.at[pl.ds(0, 2)], lambda: stat_r.at[pl.ds(2, 2)], to_pair)
    define("st1", lambda: stat_s.at[pl.ds(2, 2)], lambda: stat_r.at[pl.ds(0, 2)], to_pair)
    define("gn", lambda: gn_send, lambda: gn_recv, to_pair)
    define("ro0", lambda: dq_t.at[2, pl.ds(512, 64)], lambda: ro_recv.at[0], to_pair)
    define("ro1", lambda: dq_t.at[3, pl.ds(512, 64)], lambda: ro_recv.at[1], to_pair)

    def term(yy, xx, first):
        return lambda: dkb.at[yy, xx, pl.ds(first, 288)]

    def column(d):
        return (x + d) % 4

    for d in range(4):
        sign, device = ("p", to_yp) if d in (1, 2) else ("m", to_ym)
        define(f"A1{sign}{d}", term(y2, column(d), 0), lambda d=d: ra1.at[d], device)
        define(f"A2p{d}", term(yp, column(d), 0), lambda d=d: ra2.at[0, d], to_yp)
        define(f"A2m{d}", term(ym, column(d), 0), lambda d=d: ra2.at[1, d], to_ym)
    for d, device in ((1, to_xp), (2, to_x2), (3, to_xm)):
        define(f"A3{d}", term(y, column(d), 0), lambda d=d: ra3.at[d - 1], device)
    turns = (y2, yp, ym, y)
    for i in range(4):
        to_first = to_x2 if i == 3 else (to_xp if i % 2 == 0 else to_xm)
        define(f"B1{i}", term(turns[i], x2, 288), lambda i=i: rb1.at[i], to_first)
        define(f"B2p{i}", term(turns[i], xp, 288), lambda i=i: rb2.at[i, 0], to_xp)
        define(f"B2m{i}", term(turns[i], xm, 288), lambda i=i: rb2.at[i, 1], to_xm)
    for i, device in enumerate((to_y2, to_yp, to_ym)):
        define(f"B3{i}", term(turns[i], x, 288), lambda i=i: rb3.at[i], device)

    for i in range(4):
        define(f"C0{i}", lambda i=i: up.at[i, f1], lambda i=i: uc.at[i, 0], to_core)
        define(f"C1{i}", lambda i=i: up.at[i, f3], lambda i=i: uc.at[i, 1], to_core)
        for j, device in enumerate((to_pair, to_far, to_z2)):
            define(f"Z{j}{i}", lambda i=i, j=j: uzs.at[i, j], lambda i=i, j=j: uz.at[i, j], device)
        for j, (yy, device) in enumerate(((yp, to_yp), (ym, to_ym), (y2, to_y2))):
            define(f"Y{j}{i}", lambda i=i, yy=yy: us2.at[i, yy], lambda i=i, j=j: uyr.at[i, j], device)
        for j, device in enumerate((to_xp, to_xm, to_x2)):
            define(f"X{j}{i}", lambda i=i: us3.at[i], lambda i=i, j=j: uxr.at[i, j], device)

    barrier = pltpu.get_barrier_semaphore()
    partners = (to_xp, to_xm, to_x2, to_yp, to_ym, to_y2, to_pair, to_core, to_far, to_z2)
    for partner in partners:
        pl.semaphore_signal(barrier, inc=1, device_id=partner, device_id_type=MESH)
    pairs = ((w_in, w_own), (nope_in, nope_o), (lat_in, lat), (rope_in, rope_o), (gout_in, gout_o))
    copies = [pltpu.make_async_copy(source, target, loads.at[i]) for i, (source, target) in enumerate(pairs)]
    for copy in copies:
        copy.start()
    query[:, 512:640, :] = jnp.zeros((4, 128, 512), BF16)
    keys[:, :, 512:640] = jnp.zeros((8, 256, 128), BF16)
    for copy in copies:
        copy.wait()
    kbuf[y * 4 + x] = lat[...]
    w_all[f] = w_own[...]
    pl.semaphore_wait(barrier, len(partners))

    start("wk2", "qn", "a1", "b1", "a2", "b2", "a5", "b5", "a3", "b3", "a4", "b4", "qr", "wk1")

    def place_rope(rope, s):
        for k in range(4):
            turned = jnp.transpose(rope[:, k * 128 : k * 128 + 128].astype(F32))
            lanes = slice(k * 128, k * 128 + 128)
            query[2 * s + 1, 512:576, lanes] = jnp.concatenate([turned[:64, :64], turned[64:, :64]], axis=1).astype(BF16)
            query[2 * s, 512:576, lanes] = jnp.concatenate([turned[:64, 64:], turned[64:, 64:]], axis=1).astype(BF16)

    place_rope(rope_o, 0)
    for name in ("a", "b"):
        wait(name + "1")
        start(name + "7", name + "8")
    for name in ("a", "b"):
        wait(name + "2")
        start(name + "9", name + "10")
    for name in ("a", "b"):
        wait(name + "5")
        start(name + "11", name + "12")
    start("wv2", "qg", "wv1")
    for name in ("a", "b"):
        wait(name + "3")
        start(name + "13")
    wait("wk2")
    start("wk3")
    for name in ("a", "b"):
        wait(name + "7")
        start(name + "14")
    for name in ("a", "b"):
        wait(name + "10")
        start(name + "15")
    for name in ("a", "b"):
        wait(name + "12")
        start(name + "16")

    def blocks(value, lanes):
        both = value[:, lanes]
        empty = jnp.zeros((64, 128), BF16)
        rows = []
        for half in (both[:64], both[64:]):
            rows.append(jnp.concatenate([half[:, :128], empty], axis=1))
            rows.append(jnp.concatenate([empty, half[:, 128:]], axis=1))
        return jnp.concatenate(rows, axis=0)

    def project(value, first, ref, s):
        def two_heads(k, _):
            lanes = pl.ds(pl.multiple_of(k * 256, 256), 256)
            w_lanes = pl.ds(pl.multiple_of(first + k * 256, 256), 256)
            to = pl.ds(pl.multiple_of(k * 128, 128), 128)
            out = mm_nt(w_all[:, :, w_lanes].reshape(512, 256), blocks(value, lanes)).astype(BF16)
            ref[2 * s + 1, 0:512, to] = out[:, :128]
            ref[2 * s, 0:512, to] = out[:, 128:]
            return 0

        lax.fori_loop(0, 4, two_heads, 0)

    wait("wk1", "wk3")
    wait("wv2")
    start("wv3")
    project(nope_o, 0, query, 0)
    for s in range(4):
        wk_t[:, s * 128 : s * 128 + 128] = jnp.transpose(w_all[s, :, 0:1024])
    wait("qn", "qr")
    place_rope(rope_p, 1)
    project(nope_p, 0, query, 1)

    def assemble(yy, xx):
        both = [kbuf[yy * 4 + xx + j] for j in range(2)]
        lanes = pl.ds(pl.multiple_of(yy * 256 + xx * 64, 128), 128)
        high_lanes = pl.ds(pl.multiple_of(1024 + yy * 256 + xx * 64, 128), 128)
        keys_t[:, lanes] = jnp.concatenate([b[:, :64] for b in both], axis=1)
        keys_t[:, high_lanes] = jnp.concatenate([b[:, 64:] for b in both], axis=1)
        for j in range(2):
            rows = slice((xx + j) * 64, (xx + j) * 64 + 64)
            main = jnp.transpose(both[j][:512])
            rest = jnp.transpose(both[j][512:])
            keys[yy, rows, 0:512] = main[:64]
            keys[yy, rows, 512:576] = rest[:64]
            keys[4 + yy, rows, 0:512] = main[64:]
            keys[4 + yy, rows, 512:576] = rest[64:]

    def key_row(yy, *names):
        wait(*names)
        assemble(yy, 0)
        assemble(yy, 2)

    key_row(y, "b4", "b13")
    key_row(yp, "a4", "a8", "b9", "b15")
    key_row(ym, "a9", "a11", "b8", "b14")
    wait("wv1", "wv3")
    project(gout_o, 1024, grad, 0)
    key_row(y2, "a13", "a14", "a15", "a16", "b11", "b16")

    peak[...] = jnp.full((4, 1, 512), NEG_START, F32)
    total[...] = jnp.zeros((4, 1, 512), F32)
    centre[...] = jnp.zeros((4, 1, 512), F32)
    relative = lax.broadcasted_iota(jnp.int32, (64, 512), 0) - lax.broadcasted_iota(jnp.int32, (64, 512), 1) % 64

    def visit(t, g, high, masked, first):
        tile = 4 + t if high else t
        slot = 16 + (g // 2) * 4 + t if high else g * 4 + t
        scores = mm(keys[tile], query[g])
        grad_probs = mm(keys[tile, :, 0:512], grad[g])
        if masked:
            block = 63 - first if high else first
            parts = []
            for xx in range(4):
                key_first = order[0, (t * 2 + zl) * 4 + xx]
                key_block = 63 - key_first if high else key_first
                parts.append(relative <= (block - key_block) * 64)
            scores = jnp.where(jnp.concatenate(parts, axis=0), scores, NEG_FILL)
        old = peak[g]
        new = jnp.maximum(old, jnp.max(scores, axis=0, keepdims=True))
        weights = jnp.exp2((scores - new) * BASE2)
        factor = jnp.exp2((old - new) * BASE2)
        total[g] = total[g] * factor + jnp.sum(weights, axis=0, keepdims=True)
        centre[g] = centre[g] * factor + jnp.sum(weights * grad_probs, axis=0, keepdims=True)
        peak[g] = new
        probs[slot] = weights.astype(BF16)
        gprob[slot] = grad_probs
        peaks[slot] = new

    def visits(s, first):
        def step(t, _):
            visit(t, 2 * s, False, False, first)
            visit(t, 2 * s + 1, False, True, first)
            visit(t, 2 * s, True, True, first)
            return 0

        lax.fori_loop(0, 4, step, 0)
        for g in (2 * s, 2 * s + 1):
            stat_s[g, 0:1] = peak[g]
            stat_s[g, 1:2] = total[g]
            stat_s[g, 2:3] = centre[g]
        start(f"st{s}")

    visits(0, order[0, blk])
    wait("qg")
    project(gout_p, 1024, grad, 1)
    visits(1, order[0, pair_blk])

    def normalise(slot, g):
        factor = jnp.exp2((peaks[slot] - peak[g]) * BASE2) / total[g]
        p = probs[slot].astype(F32) * factor
        probs[slot] = p.astype(BF16)
        gscore[slot] = (p * (gprob[slot] - centre[g]) * SCALE).astype(BF16)

    def merge(s):
        wait(f"st{1 - s}")
        for g in (2 * s, 2 * s + 1):
            here, there = stat_s[g], stat_r[g]
            new = jnp.maximum(here[0:1], there[0:1])
            f_here = jnp.exp2((here[0:1] - new) * BASE2)
            f_there = jnp.exp2((there[0:1] - new) * BASE2)
            norm = here[1:2] * f_here + there[1:2] * f_there
            peak[g] = new
            total[g] = norm
            centre[g] = (here[2:3] * f_here + there[2:3] * f_there) / norm

        def low_slots(i, _):
            normalise(s * 8 + i, 2 * s + i // 4)
            return 0

        def high_slots(i, _):
            normalise(16 + s * 4 + i, 2 * s)
            return 0

        lax.fori_loop(0, 8, low_slots, 0)
        lax.fori_loop(0, 4, high_slots, 0)

    def times_keys(ref, rows, source, s, lanes):
        low = source[8 * s : 8 * s + 4, :, lanes].reshape(1024, -1)
        high = source[16 + 4 * s : 20 + 4 * s, :, lanes].reshape(1024, -1)
        ref[2 * s, :, lanes] = mm(keys_t[rows, :], jnp.concatenate([low, high], axis=0)).astype(BF16)
        low = source[8 * s + 4 : 8 * s + 8, :, lanes].reshape(1024, -1)
        ref[2 * s + 1, :, lanes] = mm(keys_t[rows, 0:1024], low).astype(BF16)

    def two_heads_rows(own, pair, k):
        lanes = slice(k * 256, k * 256 + 256)
        mine, other = blocks(own, lanes), blocks(pair, lanes)
        return jnp.concatenate([mine[128:], mine[:128], other[128:], other[:128]], axis=0)

    def weight_terms(i, ref, own, pair):
        for j in range(2):
            k = (i % 2) * 2 + j
            left = jnp.concatenate([ref[g, 0:512, k * 128 : k * 128 + 128] for g in range(4)], axis=1)
            whole = mm(left, two_heads_rows(own, pair, k))
            up[i, :, :, j * 256 : j * 256 + 256] = whole.astype(BF16).reshape(4, 128, 256)
        start(f"C0{i}", f"C1{i}")

    def sum_core(i):
        wait(f"C0{i}", f"C1{i}")
        for j, (shard, slot, plane) in enumerate(((f, 0, 1 - zl), (f2, 1, 1 - zl), (f2, 1, zl))):
            for yy in range(4):
                rows = pl.ds(pl.multiple_of(yy * 32 + plane * 16, 16), 16)
                whole = up[i, shard, rows].astype(F32) + uc[i, slot, rows].astype(F32)
                uzs[i, j, yy] = whole.astype(BF16)
        start(f"Z0{i}", f"Z1{i}", f"Z2{i}")

    def sum_z(i):
        wait(f"Z0{i}", f"Z1{i}", f"Z2{i}")
        for yy in range(4):
            rows = pl.ds(pl.multiple_of(yy * 32 + zl * 16, 16), 16)
            whole = up[i, f, rows].astype(F32) + uc[i, 0, rows].astype(F32)
            for j in range(3):
                whole = whole + uz[i, j, yy].astype(F32)
            us2[i, yy] = whole.astype(BF16)
        start(f"Y0{i}", f"Y1{i}", f"Y2{i}")

    def sum_y(i):
        wait(f"Y0{i}", f"Y1{i}", f"Y2{i}")
        whole = us2[i, y].astype(F32) + uyr[i, 0].astype(F32) + uyr[i, 1].astype(F32) + uyr[i, 2].astype(F32)
        us3[i] = whole.astype(BF16)
        start(f"X0{i}", f"X1{i}", f"X2{i}")

    def sum_x(i):
        wait(f"X0{i}", f"X1{i}", f"X2{i}")
        whole = us3[i].astype(F32) + uxr[i, 0].astype(F32) + uxr[i, 1].astype(F32) + uxr[i, 2].astype(F32)
        mine_rows = whole[0:4]
        for xx in range(1, 4):
            mine_rows = jnp.where(x == xx, whole[xx * 4 : xx * 4 + 4], mine_rows)
        first = (1024, 1536, 0, 512)[i]
        gu_out[:, first : first + 512] = mine_rows

    def back(s, ref):
        def two_heads(k, _):
            lanes = pl.ds(pl.multiple_of(k * 128, 128), 128)
            rows = pl.ds(pl.multiple_of(k * 256, 256), 256)
            left = jnp.concatenate([dq_t[2 * s + 1, 0:512, lanes], dq_t[2 * s, 0:512, lanes]], axis=1)
            out = mm(wk_t[rows, :], left)
            ref[pl.ds(pl.multiple_of(k * 256, 256), 128), :] = jnp.concatenate(
                [out[:128, 0:64], out[:128, 128:192]], axis=1
            ).astype(ref.dtype)
            ref[pl.ds(pl.multiple_of(k * 256 + 128, 128), 128), :] = jnp.concatenate(
                [out[128:, 64:128], out[128:, 192:256]], axis=1
            ).astype(ref.dtype)
            return 0

        lax.fori_loop(0, 4, two_heads, 0)

    def key_tile(t):
        def one(slots):
            a = sum(mm_nt(query[g, 0:576], gscore[slot]) for g, slot in slots)
            b = sum(mm_nt(grad[g], probs[slot]) for g, slot in slots)
            return a[:512] + b, a[512:]

        low, low_rest = one([(g, g * 4 + t) for g in range(4)])
        high, high_rest = one([(2 * s, 16 + s * 4 + t) for s in range(2)])
        for xx in range(4):
            lanes = slice(xx * 64, xx * 64 + 64)
            dkb[t, xx, 0:512] = jnp.concatenate([low[:, lanes], high[:, lanes]], axis=1).astype(BF16)
            dkb[t, xx, 512:576] = jnp.concatenate([low_rest[:, lanes], high_rest[:, lanes]], axis=1).astype(BF16)

    upper, lower = pl.ds(0, 288), pl.ds(288, 288)

    def b_second(i):
        wait(f"B1{i}")
        add_into(dkb.at[turns[i], xp if i % 2 == 0 else xm, lower], rb1.at[i])
        start(f"B2p{i}", f"B2m{i}")

    def b_last(i):
        wait(f"B2p{i}", f"B2m{i}")
        add_into(dkb.at[turns[i], x, lower], rb2.at[i, 0], rb2.at[i, 1])
        start(f"B3{i}")

    every, halves = slice(0, 512), (slice(0, 256), slice(256, 512))
    main, full = slice(0, 512), slice(0, 576)
    merge(1)
    times_keys(out_t, main, probs, 1, every)
    merge(0)
    times_keys(out_t, main, probs, 0, halves[0])
    weight_terms(0, out_t, gout_o, gout_p)
    times_keys(out_t, main, probs, 0, halves[1])
    weight_terms(1, out_t, gout_o, gout_p)
    key_tile(y2)
    start("A1p2", "A1m3", "A1p1", "A1m0", "B10")
    sum_core(0)
    sum_core(1)
    times_keys(dq_t, full, gscore, 1, every)
    back(1, gn_send)
    start("ro0", "ro1", "gn")
    times_keys(dq_t, full, gscore, 0, halves[0])
    weight_terms(2, dq_t, nope_o, nope_p)
    b_second(0)
    times_keys(dq_t, full, gscore, 0, halves[1])
    weight_terms(3, dq_t, nope_o, nope_p)
    sum_core(2)
    sum_z(0)

    def key_turn(i, _):
        key_tile((y + jnp.where(i == 1, 1, jnp.where(i == 2, 3, 0))) % 4)

        @pl.when(i == 1)
        def _():
            for d in (2, 1):
                wait(f"A1p{d}")
                add_into(dkb.at[yp, column(d), upper], ra1.at[d])
                start(f"A2p{d}")
            start("B11", "A2p3", "A2p0")
            sum_core(3)
            b_last(0)
            sum_z(1)

        @pl.when(i == 2)
        def _():
            start("A2m2", "A2m1", "B12")
            for d in (3, 0):
                wait(f"A1m{d}")
                add_into(dkb.at[ym, column(d), upper], ra1.at[d])
                start(f"A2m{d}")
            b_second(1)
            sum_y(0)

        @pl.when(i == 3)
        def _():
            start("B13", "B2p3", "B2m3")
            b_second(2)
            b_last(1)
            sum_y(1)
            sum_z(2)

        return 0

    lax.fori_loop(1, 4, key_turn, 0)
    def a_last(d):
        wait(f"A2p{d}", f"A2m{d}")
        add_into(dkb.at[y, column(d), upper], ra2.at[0, d], ra2.at[1, d])
        start(f"A3{d}")

    a_last(2)
    back(0, gn_own)
    a_last(1)
    a_last(3)
    sum_z(3)
    b_last(2)
    sum_x(0)
    sum_x(1)
    sum_y(2)

    wait("gn", "ro0", "ro1")
    gn_out[...] = jnp.transpose(gn_own[...] + gn_recv[...].astype(F32)).astype(BF16)
    for half, g in ((0, 1), (1, 0)):
        rope = jnp.transpose(dq_t[g, 512:576].astype(F32) + ro_recv[g].astype(F32))
        gr_out[half * 64 : half * 64 + 64, :] = jnp.concatenate(
            [rope[h * 64 : h * 64 + 64] for h in range(HEADS)], axis=1
        ).astype(BF16)

    sum_y(3)
    wait("A31", "A32", "A33", "A2p0", "A2m0")
    add_into(dkb.at[y, x, upper], ra2.at[0, 0], ra2.at[1, 0], ra3.at[0], ra3.at[1], ra3.at[2])
    wait("B13", "B2p3", "B2m3", "B30", "B31", "B32")
    add_into(dkb.at[y, x, lower], rb1.at[3], rb2.at[3, 0], rb2.at[3, 1], rb3.at[0], rb3.at[1], rb3.at[2])
    gl_out[...] = dkb[y, x]
    sum_x(2)
    sum_x(3)
    for name in made:
        made[name]().wait_send()


def hand_over(*refs):
    for source, target in zip(refs[:4], refs[4:]):
        target[...] = source[...]


def per_device(query_nope, query_rope, latent, grad_out, w_up, block_order):
    shapes = [
        ((16, 576, 128), BF16), ((8, 256, 640), BF16), ((576, 2048), BF16),
        ((128, 1024), BF16), ((128, 512), BF16), ((128, 1024), BF16), ((4, 128, 2048), BF16), ((1024, 512), BF16),
        ((4, 640, 512), BF16), ((4, 512, 512), BF16), ((24, 256, 512), BF16), ((24, 256, 512), F32), ((24, 256, 512), BF16),
        ((24, 1, 512), F32), ((4, 1, 512), F32), ((4, 1, 512), F32), ((4, 1, 512), F32), ((4, 8, 512), F32), ((4, 8, 512), F32),
        ((4, 576, 512), BF16), ((4, 512, 512), BF16), ((1024, 128), F32), ((1024, 128), BF16), ((1024, 128), BF16), ((2, 64, 512), BF16),
        ((4, 4, 576, 128), BF16), ((4, 288, 128), BF16), ((2, 4, 288, 128), BF16), ((3, 288, 128), BF16),
        ((4, 288, 128), BF16), ((4, 2, 288, 128), BF16), ((3, 288, 128), BF16),
        ((4, 4, 128, 512), BF16), ((4, 2, 128, 512), BF16), ((4, 3, 4, 16, 512), BF16), ((4, 3, 4, 16, 512), BF16),
        ((4, 4, 16, 512), BF16), ((4, 3, 16, 512), BF16), ((4, 16, 512), BF16), ((4, 3, 16, 512), BF16),
        ((576, 128), BF16), ((128, 1024), BF16), ((128, 512), BF16), ((128, 1024), BF16), ((128, 2048), BF16),
    ]
    vmem = pl.BlockSpec(memory_space=pltpu.VMEM)
    gn, gr, gl, gu = pl.pallas_call(
        kernel,
        out_shape=(
            jax.ShapeDtypeStruct((128, 1024), BF16),
            jax.ShapeDtypeStruct((128, 512), BF16),
            jax.ShapeDtypeStruct((576, 128), BF16),
            jax.ShapeDtypeStruct((4, 2048), F32),
        ),
        in_specs=[pl.BlockSpec(memory_space=pltpu.SMEM)] + [pl.BlockSpec(memory_space=pl.ANY)] * 5,
        out_specs=(vmem,) * 4,
        scratch_shapes=[pltpu.VMEM(shape, dtype) for shape, dtype in shapes]
        + [pltpu.SemaphoreType.DMA((5,)), pltpu.SemaphoreType.DMA((COPIES,)), pltpu.SemaphoreType.DMA((COPIES,))],
        compiler_params=pltpu.CompilerParams(
            collective_id=0, has_side_effects=True, vmem_limit_bytes=63 * 1024 * 1024
        ),
        name="latent_attention_backward",
    )(block_order.T, latent[0].T, query_nope[0], query_rope[0], grad_out[0], w_up)
    gn, gr, gl, gu = pl.pallas_call(
        hand_over,
        out_shape=tuple(jax.ShapeDtypeStruct(a.shape, a.dtype) for a in (gn, gr, gl, gu)),
        in_specs=[vmem] * 4,
        out_specs=(vmem,) * 4,
        name="hand_over",
    )(gn, gr, gl, gu)
    return gn[None], gr[None], gl.T[None], gu


def solution(mesh):
    rows = P("fsdp", "blk", None)
    return jax.shard_map(
        per_device,
        mesh=mesh,
        in_specs=(rows, rows, rows, rows, P("fsdp", None), P()),
        out_specs=(rows, rows, rows, P(("fsdp", "blk"), None)),
        check_vma=False,
    )
```

```python
import functools
import math

import jax
import jax.numpy as jnp
from jax import lax
from jax.experimental import pallas as pl
from jax.experimental.pallas import tpu as pltpu
from jax.sharding import PartitionSpec as P

HEADS = 8
LATENT = 512
SCALE = 1.0 / math.sqrt(192.0)
NEG_FILL = -1e30
NEG_START = -1e20
BASE2 = SCALE * math.log2(math.e)
F32 = jnp.float32
BF16 = jnp.bfloat16
MESH = pl.DeviceIdType.MESH
COPIES = 144


def mm(a, b):
    return lax.dot_general(a, b, (((1,), (0,)), ((), ())), preferred_element_type=F32)


def mm_nt(a, b):
    return lax.dot_general(a, b, (((1,), (1,)), ((), ())), preferred_element_type=F32)


def add_into(ref, *others):
    total = ref[...].astype(F32)
    for other in others:
        total = total + other[...].astype(F32)
    ref[...] = total.astype(BF16)


def kernel(
    order, lat_in, nope_in, rope_in, gout_in, w_in,
    gn_out, gr_out, gl_out, gu_out,
    kbuf, keys, keys_t, nope_p, rope_p, gout_p, w_all, wk_t,
    query, grad, probs, gprob, gscore, peaks, peak, total, centre, stat_s, stat_r,
    dq_t, out_t, gn_own, gn_send, gn_recv, ro_recv,
    dkb, ra1, ra2, ra3, rb1, rb2, rb3,
    up, uc, uzs, uz, us2, uyr, us3, uxr,
    lat, nope_o, rope_o, gout_o, w_own, loads,
    send, recv,
):
    f = lax.axis_index("fsdp")
    blk = lax.axis_index("blk")
    x, zl, y = blk % 4, (blk // 4) % 2, blk // 8
    xp, xm, x2 = (x + 1) % 4, (x + 3) % 4, (x + 2) % 4
    yp, ym, y2 = (y + 1) % 4, (y + 3) % 4, (y + 2) % 4
    f1 = f + 1 - 2 * (f % 2)
    f2 = (f + 2) % 4
    f3 = (f1 + 2) % 4
    pair_blk = blk + 4 - 8 * zl

    def at(yy, xx):
        return {"blk": (yy * 2 + zl) * 4 + xx}

    to_xp, to_xm, to_x2 = at(y, xp), at(y, xm), at(y, x2)
    to_yp, to_ym, to_y2 = at(yp, x), at(ym, x), at(y2, x)
    to_pair = {"blk": pair_blk}
    to_core = {"fsdp": f1}
    to_far = {"fsdp": f2, "blk": pair_blk}
    to_z2 = {"fsdp": f2}

    made = {}

    def define(name, src, dst, device):
        number = len(made)
        made[name] = lambda: pltpu.make_async_remote_copy(
            src_ref=src(), dst_ref=dst(), send_sem=send.at[number], recv_sem=recv.at[number],
            device_id=device, device_id_type=MESH,
        )

    def start(*names):
        for name in names:
            made[name]().start()

    def wait(*names):
        for name in names:
            made[name]().wait_recv()

    def same(name, part, device):
        define(name, part, part, device)

    for name, first, swap in (("a", 0, False), ("b", 288, True)):
        def part(dy, dx, first=first, swap=swap):
            if swap:
                dy, dx = dx, dy
            return lambda: kbuf.at[((y + dy) % 4) * 4 + (x + dx) % 4, pl.ds(first, 288)]

        if swap:
            ip, im, i2, jp, jm = to_yp, to_ym, to_y2, to_xp, to_xm
        else:
            ip, im, i2, jp, jm = to_xp, to_xm, to_x2, to_yp, to_ym
        same(name + "1", part(0, 0), ip)
        same(name + "2", part(0, 0), im)
        same(name + "5", part(0, 0), i2)
        same(name + "3", part(0, 0), jp)
        same(name + "4", part(0, 0), jm)
        same(name + "7", part(0, 3), jp)
        same(name + "8", part(0, 3), jm)
        same(name + "9", part(0, 1), jp)
        same(name + "10", part(0, 1), jm)
        same(name + "11", part(0, 2), jp)
        same(name + "12", part(0, 2), jm)
        same(name + "13", part(3, 0), jp)
        same(name + "14", part(3, 3), jp)
        same(name + "15", part(1, 1), jm)
        same(name + "16", part(1, 2), jm)

    define("qn", lambda: nope_o, lambda: nope_p, to_pair)
    define("qr", lambda: rope_o, lambda: rope_p, to_pair)
    define("qg", lambda: gout_o, lambda: gout_p, to_pair)
    for name, first in (("k", 0), ("v", 1024)):
        def own_w(first=first):
            return w_own.at[:, pl.ds(first, 1024)]

        def far_w(shard, first=first):
            return lambda: w_all.at[shard, :, pl.ds(first, 1024)]

        define(f"w{name}1", own_w, far_w(f), to_core)
        define(f"w{name}2", own_w, far_w(f), to_far)
        define(f"w{name}3", far_w(f2), far_w(f2), to_core)
    define("st0", lambda: stat_s.at[pl.ds(0, 2)], lambda: stat_r.at[pl.ds(2, 2)], to_pair)
    define("st1", lambda: stat_s.at[pl.ds(2, 2)], lambda: stat_r.at[pl.ds(0, 2)], to_pair)
    define("gn", lambda: gn_send, lambda: gn_recv, to_pair)
    define("ro0", lambda: dq_t.at[2, pl.ds(512, 64)], lambda: ro_recv.at[0], to_pair)
    define("ro1", lambda: dq_t.at[3, pl.ds(512, 64)], lambda: ro_recv.at[1], to_pair)

    def term(yy, xx, first):
        return lambda: dkb.at[yy, xx, pl.ds(first, 288)]

    def column(d):
        return (x + d) % 4

    for d in range(4):
        sign, device = ("p", to_yp) if d in (1, 2) else ("m", to_ym)
        define(f"A1{sign}{d}", term(y2, column(d), 0), lambda d=d: ra1.at[d], device)
        define(f"A2p{d}", term(yp, column(d), 0), lambda d=d: ra2.at[0, d], to_yp)
        define(f"A2m{d}", term(ym, column(d), 0), lambda d=d: ra2.at[1, d], to_ym)
    for d, device in ((1, to_xp), (2, to_x2), (3, to_xm)):
        define(f"A3{d}", term(y, column(d), 0), lambda d=d: ra3.at[d - 1], device)
    turns = (y2, yp, ym, y)
    for i in range(4):
        define(f"B1{i}", term(turns[i], x2, 288), lambda i=i: rb1.at[i], to_x2)
        define(f"B2p{i}", term(turns[i], xp, 288), lambda i=i: rb2.at[i, 0], to_xp)
        define(f"B2m{i}", term(turns[i], xm, 288), lambda i=i: rb2.at[i, 1], to_xm)
    for i, device in enumerate((to_y2, to_yp, to_ym)):
        define(f"B3{i}", term(turns[i], x, 288), lambda i=i: rb3.at[i], device)

    for i in range(4):
        define(f"C0{i}", lambda i=i: up.at[i, f1], lambda i=i: uc.at[i, 0], to_core)
        define(f"C1{i}", lambda i=i: up.at[i, f3], lambda i=i: uc.at[i, 1], to_core)
        for j, device in enumerate((to_pair, to_far, to_z2)):
            define(f"Z{j}{i}", lambda i=i, j=j: uzs.at[i, j], lambda i=i, j=j: uz.at[i, j], device)
        for j, (yy, device) in enumerate(((yp, to_yp), (ym, to_ym), (y2, to_y2))):
            define(f"Y{j}{i}", lambda i=i, yy=yy: us2.at[i, yy], lambda i=i, j=j: uyr.at[i, j], device)
        for j, device in enumerate((to_xp, to_xm, to_x2)):
            define(f"X{j}{i}", lambda i=i: us3.at[i], lambda i=i, j=j: uxr.at[i, j], device)

    barrier = pltpu.get_barrier_semaphore()
    partners = (to_xp, to_xm, to_x2, to_yp, to_ym, to_y2, to_pair, to_core, to_far, to_z2)
    for partner in partners:
        pl.semaphore_signal(barrier, inc=1, device_id=partner, device_id_type=MESH)
    pairs = ((w_in, w_own), (nope_in, nope_o), (lat_in, lat), (rope_in, rope_o), (gout_in, gout_o))
    copies = [pltpu.make_async_copy(source, target, loads.at[i]) for i, (source, target) in enumerate(pairs)]
    for copy in copies:
        copy.start()
    query[:, 512:640, :] = jnp.zeros((4, 128, 512), BF16)
    keys[:, :, 512:640] = jnp.zeros((8, 256, 128), BF16)
    for copy in copies:
        copy.wait()
    kbuf[y * 4 + x] = lat[...]
    w_all[f] = w_own[...]
    pl.semaphore_wait(barrier, len(partners))

    start("wk2", "qn", "wv2", "a1", "b1", "a2", "b2", "a5", "b5", "a3", "b3", "a4", "b4", "qr", "wk1")

    def place_rope(rope, s):
        for k in range(4):
            turned = jnp.transpose(rope[:, k * 128 : k * 128 + 128].astype(F32))
            lanes = slice(k * 128, k * 128 + 128)
            query[2 * s + 1, 512:576, lanes] = jnp.concatenate([turned[:64, :64], turned[64:, :64]], axis=1).astype(BF16)
            query[2 * s, 512:576, lanes] = jnp.concatenate([turned[:64, 64:], turned[64:, 64:]], axis=1).astype(BF16)

    place_rope(rope_o, 0)
    for name in ("a", "b"):
        wait(name + "1")
        start(name + "7", name + "8")
    for name in ("a", "b"):
        wait(name + "2")
        start(name + "9", name + "10")
    for name in ("a", "b"):
        wait(name + "5")
        start(name + "11", name + "12")
    start("qg", "wv1")
    for name in ("a", "b"):
        wait(name + "3")
        start(name + "13")
    wait("wk2")
    start("wk3")
    for name in ("a", "b"):
        wait(name + "7")
        start(name + "14")
    for name in ("a", "b"):
        wait(name + "10")
        start(name + "15")
    for name in ("a", "b"):
        wait(name + "12")
        start(name + "16")

    def blocks(value, lanes):
        both = value[:, lanes]
        empty = jnp.zeros((64, 128), BF16)
        rows = []
        for half in (both[:64], both[64:]):
            rows.append(jnp.concatenate([half[:, :128], empty], axis=1))
            rows.append(jnp.concatenate([empty, half[:, 128:]], axis=1))
        return jnp.concatenate(rows, axis=0)

    def project(value, first, ref, s):
        def two_heads(k, _):
            lanes = pl.ds(pl.multiple_of(k * 256, 256), 256)
            w_lanes = pl.ds(pl.multiple_of(first + k * 256, 256), 256)
            to = pl.ds(pl.multiple_of(k * 128, 128), 128)
            out = mm_nt(w_all[:, :, w_lanes].reshape(512, 256), blocks(value, lanes)).astype(BF16)
            ref[2 * s + 1, 0:512, to] = out[:, :128]
            ref[2 * s, 0:512, to] = out[:, 128:]
            return 0

        lax.fori_loop(0, 4, two_heads, 0)

    wait("wk1", "wk3")
    wait("wv2")
    start("wv3")
    project(nope_o, 0, query, 0)
    for s in range(4):
        wk_t[:, s * 128 : s * 128 + 128] = jnp.transpose(w_all[s, :, 0:1024])
    wait("qn", "qr")
    place_rope(rope_p, 1)
    project(nope_p, 0, query, 1)

    def assemble(yy, xx):
        both = [kbuf[yy * 4 + xx + j] for j in range(2)]
        lanes = pl.ds(pl.multiple_of(yy * 256 + xx * 64, 128), 128)
        high_lanes = pl.ds(pl.multiple_of(1024 + yy * 256 + xx * 64, 128), 128)
        keys_t[:, lanes] = jnp.concatenate([b[:, :64] for b in both], axis=1)
        keys_t[:, high_lanes] = jnp.concatenate([b[:, 64:] for b in both], axis=1)
        for j in range(2):
            rows = slice((xx + j) * 64, (xx + j) * 64 + 64)
            main = jnp.transpose(both[j][:512])
            rest = jnp.transpose(both[j][512:])
            keys[yy, rows, 0:512] = main[:64]
            keys[yy, rows, 512:576] = rest[:64]
            keys[4 + yy, rows, 0:512] = main[64:]
            keys[4 + yy, rows, 512:576] = rest[64:]

    def key_row(yy, *names):
        wait(*names)
        assemble(yy, 0)
        assemble(yy, 2)

    key_row(y, "b4", "b13")
    key_row(yp, "a4", "a8", "b9", "b15")
    key_row(ym, "a9", "a11", "b8", "b14")
    wait("wv1", "wv3")
    project(gout_o, 1024, grad, 0)
    peak[...] = jnp.full((4, 1, 512), NEG_START, F32)
    total[...] = jnp.zeros((4, 1, 512), F32)
    centre[...] = jnp.zeros((4, 1, 512), F32)
    relative = lax.broadcasted_iota(jnp.int32, (64, 512), 0) - lax.broadcasted_iota(jnp.int32, (64, 512), 1) % 64

    def visit(t, g, high, masked, first):
        tile = 4 + t if high else t
        slot = 16 + (g // 2) * 4 + t if high else g * 4 + t
        scores = mm(keys[tile], query[g])
        grad_probs = mm(keys[tile, :, 0:512], grad[g])
        if masked:
            block = 63 - first if high else first
            parts = []
            for xx in range(4):
                key_first = order[0, (t * 2 + zl) * 4 + xx]
                key_block = 63 - key_first if high else key_first
                parts.append(relative <= (block - key_block) * 64)
            scores = jnp.where(jnp.concatenate(parts, axis=0), scores, NEG_FILL)
        old = peak[g]
        new = jnp.maximum(old, jnp.max(scores, axis=0, keepdims=True))
        weights = jnp.exp2((scores - new) * BASE2)
        factor = jnp.exp2((old - new) * BASE2)
        total[g] = total[g] * factor + jnp.sum(weights, axis=0, keepdims=True)
        centre[g] = centre[g] * factor + jnp.sum(weights * grad_probs, axis=0, keepdims=True)
        peak[g] = new
        probs[slot] = weights.astype(BF16)
        gprob[slot] = grad_probs
        peaks[slot] = new

    def visits(s, first, begin, end):
        def step(i, _):
            t = (y + jnp.where(i == 0, 0, jnp.where(i == 1, 1, jnp.where(i == 2, 3, 2)))) % 4
            visit(t, 2 * s, False, False, first)
            visit(t, 2 * s + 1, False, True, first)
            visit(t, 2 * s, True, True, first)
            return 0

        lax.fori_loop(begin, end, step, 0)

    def tell(s):
        for g in (2 * s, 2 * s + 1):
            stat_s[g, 0:1] = peak[g]
            stat_s[g, 1:2] = total[g]
            stat_s[g, 2:3] = centre[g]
        start(f"st{s}")

    visits(0, order[0, blk], 0, 3)
    key_row(y2, "a13", "a14", "a15", "a16", "b11", "b16")
    visits(0, order[0, blk], 3, 4)
    tell(0)
    wait("qg")
    project(gout_p, 1024, grad, 1)
    visits(1, order[0, pair_blk], 0, 4)
    tell(1)

    def normalise(slot, g):
        factor = jnp.exp2((peaks[slot] - peak[g]) * BASE2) / total[g]
        p = probs[slot].astype(F32) * factor
        probs[slot] = p.astype(BF16)
        gscore[slot] = (p * (gprob[slot] - centre[g]) * SCALE).astype(BF16)

    def merge(s):
        wait(f"st{1 - s}")
        for g in (2 * s, 2 * s + 1):
            here, there = stat_s[g], stat_r[g]
            new = jnp.maximum(here[0:1], there[0:1])
            f_here = jnp.exp2((here[0:1] - new) * BASE2)
            f_there = jnp.exp2((there[0:1] - new) * BASE2)
            norm = here[1:2] * f_here + there[1:2] * f_there
            peak[g] = new
            total[g] = norm
            centre[g] = (here[2:3] * f_here + there[2:3] * f_there) / norm

        def low_slots(i, _):
            normalise(s * 8 + i, 2 * s + i // 4)
            return 0

        def high_slots(i, _):
            normalise(16 + s * 4 + i, 2 * s)
            return 0

        lax.fori_loop(0, 8, low_slots, 0)
        lax.fori_loop(0, 4, high_slots, 0)

    def times_keys(ref, rows, source, s, lanes):
        low = source[8 * s : 8 * s + 4, :, lanes].reshape(1024, -1)
        high = source[16 + 4 * s : 20 + 4 * s, :, lanes].reshape(1024, -1)
        ref[2 * s, :, lanes] = mm(keys_t[rows, :], jnp.concatenate([low, high], axis=0)).astype(BF16)
        low = source[8 * s + 4 : 8 * s + 8, :, lanes].reshape(1024, -1)
        ref[2 * s + 1, :, lanes] = mm(keys_t[rows, 0:1024], low).astype(BF16)

    def two_heads_rows(own, pair, k):
        lanes = slice(k * 256, k * 256 + 256)
        mine, other = blocks(own, lanes), blocks(pair, lanes)
        return jnp.concatenate([mine[128:], mine[:128], other[128:], other[:128]], axis=0)

    def weight_terms(i, ref, own, pair):
        for j in range(2):
            k = (i % 2) * 2 + j
            left = jnp.concatenate([ref[g, 0:512, k * 128 : k * 128 + 128] for g in range(4)], axis=1)
            whole = mm(left, two_heads_rows(own, pair, k))
            up[i, :, :, j * 256 : j * 256 + 256] = whole.astype(BF16).reshape(4, 128, 256)
        start(f"C0{i}", f"C1{i}")

    def sum_core(i):
        wait(f"C0{i}", f"C1{i}")
        for j, (shard, slot, plane) in enumerate(((f, 0, 1 - zl), (f2, 1, 1 - zl), (f2, 1, zl))):
            for yy in range(4):
                rows = pl.ds(pl.multiple_of(yy * 32 + plane * 16, 16), 16)
                whole = up[i, shard, rows].astype(F32) + uc[i, slot, rows].astype(F32)
                uzs[i, j, yy] = whole.astype(BF16)
        start(f"Z0{i}", f"Z1{i}", f"Z2{i}")

    def sum_z(i):
        wait(f"Z0{i}", f"Z1{i}", f"Z2{i}")
        for yy in range(4):
            rows = pl.ds(pl.multiple_of(yy * 32 + zl * 16, 16), 16)
            whole = up[i, f, rows].astype(F32) + uc[i, 0, rows].astype(F32)
            for j in range(3):
                whole = whole + uz[i, j, yy].astype(F32)
            us2[i, yy] = whole.astype(BF16)
        start(f"Y0{i}", f"Y1{i}", f"Y2{i}")

    def sum_y(i):
        wait(f"Y0{i}", f"Y1{i}", f"Y2{i}")
        whole = us2[i, y].astype(F32) + uyr[i, 0].astype(F32) + uyr[i, 1].astype(F32) + uyr[i, 2].astype(F32)
        us3[i] = whole.astype(BF16)
        start(f"X0{i}", f"X1{i}", f"X2{i}")

    def sum_x(i):
        wait(f"X0{i}", f"X1{i}", f"X2{i}")
        whole = us3[i].astype(F32) + uxr[i, 0].astype(F32) + uxr[i, 1].astype(F32) + uxr[i, 2].astype(F32)
        mine_rows = whole[0:4]
        for xx in range(1, 4):
            mine_rows = jnp.where(x == xx, whole[xx * 4 : xx * 4 + 4], mine_rows)
        first = (1024, 1536, 0, 512)[i]
        gu_out[:, first : first + 512] = mine_rows

    def back(s, ref):
        def two_heads(k, _):
            lanes = pl.ds(pl.multiple_of(k * 128, 128), 128)
            rows = pl.ds(pl.multiple_of(k * 256, 256), 256)
            left = jnp.concatenate([dq_t[2 * s + 1, 0:512, lanes], dq_t[2 * s, 0:512, lanes]], axis=1)
            out = mm(wk_t[rows, :], left)
            ref[pl.ds(pl.multiple_of(k * 256, 256), 128), :] = jnp.concatenate(
                [out[:128, 0:64], out[:128, 128:192]], axis=1
            ).astype(ref.dtype)
            ref[pl.ds(pl.multiple_of(k * 256 + 128, 128), 128), :] = jnp.concatenate(
                [out[128:, 64:128], out[128:, 192:256]], axis=1
            ).astype(ref.dtype)
            return 0

        lax.fori_loop(0, 4, two_heads, 0)

    def key_tile(t):
        def one(slots):
            a = sum(mm_nt(query[g, 0:576], gscore[slot]) for g, slot in slots)
            b = sum(mm_nt(grad[g], probs[slot]) for g, slot in slots)
            return a[:512] + b, a[512:]

        low, low_rest = one([(g, g * 4 + t) for g in range(4)])
        high, high_rest = one([(2 * s, 16 + s * 4 + t) for s in range(2)])
        for xx in range(4):
            lanes = slice(xx * 64, xx * 64 + 64)
            dkb[t, xx, 0:512] = jnp.concatenate([low[:, lanes], high[:, lanes]], axis=1).astype(BF16)
            dkb[t, xx, 512:576] = jnp.concatenate([low_rest[:, lanes], high_rest[:, lanes]], axis=1).astype(BF16)

    upper, lower = pl.ds(0, 288), pl.ds(288, 288)

    def b_first(i):
        start(f"B1{i}", f"B2p{i}", f"B2m{i}")

    def b_last(i):
        wait(f"B1{i}", f"B2p{i}", f"B2m{i}")
        add_into(dkb.at[turns[i], x, lower], rb1.at[i], rb2.at[i, 0], rb2.at[i, 1])
        start(f"B3{i}")

    every, halves = slice(0, 512), (slice(0, 256), slice(256, 512))
    main, full = slice(0, 512), slice(0, 576)
    def a_second(d, row, sign):
        wait(f"A1{sign}{d}")
        add_into(dkb.at[row, column(d), upper], ra1.at[d])
        start(f"A2{sign}{d}")

    merge(1)
    times_keys(out_t, main, probs, 1, every)
    merge(0)

    def first_turn(i, _):
        key_tile((y + 2 - i) % 4)

        @pl.when(i == 0)
        def _():
            start("A1p2", "A1m3", "A1p1", "A1m0")
            b_first(0)

        return 0

    lax.fori_loop(0, 2, first_turn, 0)
    start("A2p3", "A2p0")
    b_first(1)
    times_keys(dq_t, full, gscore, 1, every)
    back(1, gn_send)
    start("ro0", "ro1", "gn")
    a_second(2, yp, "p")
    a_second(1, yp, "p")
    times_keys(out_t, main, probs, 0, halves[0])
    weight_terms(0, out_t, gout_o, gout_p)
    times_keys(out_t, main, probs, 0, halves[1])
    weight_terms(1, out_t, gout_o, gout_p)
    sum_core(0)
    b_last(0)
    times_keys(dq_t, full, gscore, 0, halves[0])
    weight_terms(2, dq_t, nope_o, nope_p)
    sum_core(1)
    times_keys(dq_t, full, gscore, 0, halves[1])
    weight_terms(3, dq_t, nope_o, nope_p)
    sum_core(2)
    b_last(1)

    def key_turn(i, _):
        key_tile((y + jnp.where(i == 2, 3, 0)) % 4)

        @pl.when(i == 2)
        def _():
            start("A2m2", "A2m1")
            b_first(2)
            sum_core(3)
            a_second(3, ym, "m")
            a_second(0, ym, "m")
            sum_z(0)
            sum_z(1)

        return 0

    lax.fori_loop(2, 4, key_turn, 0)
    b_first(3)

    def a_last(d):
        wait(f"A2p{d}", f"A2m{d}")
        add_into(dkb.at[y, column(d), upper], ra2.at[0, d], ra2.at[1, d])
        start(f"A3{d}")

    sum_z(2)
    a_last(2)
    sum_z(3)
    a_last(1)
    a_last(3)
    b_last(2)
    sum_y(0)
    sum_y(1)
    sum_y(2)
    sum_y(3)
    back(0, gn_own)
    sum_x(0)
    sum_x(1)

    wait("gn", "ro0", "ro1")
    gn_out[...] = jnp.transpose(gn_own[...] + gn_recv[...].astype(F32)).astype(BF16)
    for half, g in ((0, 1), (1, 0)):
        rope = jnp.transpose(dq_t[g, 512:576].astype(F32) + ro_recv[g].astype(F32))
        gr_out[half * 64 : half * 64 + 64, :] = jnp.concatenate(
            [rope[h * 64 : h * 64 + 64] for h in range(HEADS)], axis=1
        ).astype(BF16)

    wait("A31", "A32", "A33", "A2p0", "A2m0")
    add_into(dkb.at[y, x, upper], ra2.at[0, 0], ra2.at[1, 0], ra3.at[0], ra3.at[1], ra3.at[2])
    wait("B13", "B2p3", "B2m3", "B30", "B31", "B32")
    add_into(dkb.at[y, x, lower], rb1.at[3], rb2.at[3, 0], rb2.at[3, 1], rb3.at[0], rb3.at[1], rb3.at[2])
    gl_out[...] = dkb[y, x]
    sum_x(2)
    sum_x(3)
    for name in made:
        made[name]().wait_send()


def hand_over(*refs):
    for source, target in zip(refs[:4], refs[4:]):
        target[...] = source[...]


def per_device(query_nope, query_rope, latent, grad_out, w_up, block_order):
    shapes = [
        ((16, 576, 128), BF16), ((8, 256, 640), BF16), ((576, 2048), BF16),
        ((128, 1024), BF16), ((128, 512), BF16), ((128, 1024), BF16), ((4, 128, 2048), BF16), ((1024, 512), BF16),
        ((4, 640, 512), BF16), ((4, 512, 512), BF16), ((24, 256, 512), BF16), ((24, 256, 512), F32), ((24, 256, 512), BF16),
        ((24, 1, 512), F32), ((4, 1, 512), F32), ((4, 1, 512), F32), ((4, 1, 512), F32), ((4, 8, 512), F32), ((4, 8, 512), F32),
        ((4, 576, 512), BF16), ((4, 512, 512), BF16), ((1024, 128), F32), ((1024, 128), BF16), ((1024, 128), BF16), ((2, 64, 512), BF16),
        ((4, 4, 576, 128), BF16), ((4, 288, 128), BF16), ((2, 4, 288, 128), BF16), ((3, 288, 128), BF16),
        ((4, 288, 128), BF16), ((4, 2, 288, 128), BF16), ((3, 288, 128), BF16),
        ((4, 4, 128, 512), BF16), ((4, 2, 128, 512), BF16), ((4, 3, 4, 16, 512), BF16), ((4, 3, 4, 16, 512), BF16),
        ((4, 4, 16, 512), BF16), ((4, 3, 16, 512), BF16), ((4, 16, 512), BF16), ((4, 3, 16, 512), BF16),
        ((576, 128), BF16), ((128, 1024), BF16), ((128, 512), BF16), ((128, 1024), BF16), ((128, 2048), BF16),
    ]
    vmem = pl.BlockSpec(memory_space=pltpu.VMEM)
    gn, gr, gl, gu = pl.pallas_call(
        kernel,
        out_shape=(
            jax.ShapeDtypeStruct((128, 1024), BF16),
            jax.ShapeDtypeStruct((128, 512), BF16),
            jax.ShapeDtypeStruct((576, 128), BF16),
            jax.ShapeDtypeStruct((4, 2048), F32),
        ),
        in_specs=[pl.BlockSpec(memory_space=pltpu.SMEM)] + [pl.BlockSpec(memory_space=pl.ANY)] * 5,
        out_specs=(vmem,) * 4,
        scratch_shapes=[pltpu.VMEM(shape, dtype) for shape, dtype in shapes]
        + [pltpu.SemaphoreType.DMA((5,)), pltpu.SemaphoreType.DMA((COPIES,)), pltpu.SemaphoreType.DMA((COPIES,))],
        compiler_params=pltpu.CompilerParams(
            collective_id=0, has_side_effects=True, vmem_limit_bytes=63 * 1024 * 1024
        ),
        name="latent_attention_backward",
    )(block_order.T, latent[0].T, query_nope[0], query_rope[0], grad_out[0], w_up)
    gn, gr, gl, gu = pl.pallas_call(
        hand_over,
        out_shape=tuple(jax.ShapeDtypeStruct(a.shape, a.dtype) for a in (gn, gr, gl, gu)),
        in_specs=[vmem] * 4,
        out_specs=(vmem,) * 4,
        name="hand_over",
    )(gn, gr, gl, gu)
    return gn[None], gr[None], gl.T[None], gu


def solution(mesh):
    rows = P("fsdp", "blk", None)
    return jax.shard_map(
        per_device,
        mesh=mesh,
        in_specs=(rows, rows, rows, rows, P("fsdp", None), P()),
        out_specs=(rows, rows, rows, P(("fsdp", "blk"), None)),
        check_vma=False,
    )
```

```python
import functools
import math

import jax
import jax.numpy as jnp
from jax import lax
from jax.experimental import pallas as pl
from jax.experimental.pallas import tpu as pltpu
from jax.sharding import PartitionSpec as P

HEADS = 8
LATENT = 512
SCALE = 1.0 / math.sqrt(192.0)
NEG_FILL = -1e30
NEG_START = -1e20
BASE2 = SCALE * math.log2(math.e)
F32 = jnp.float32
BF16 = jnp.bfloat16
MESH = pl.DeviceIdType.MESH
COPIES = 144


def mm(a, b):
    return lax.dot_general(a, b, (((1,), (0,)), ((), ())), preferred_element_type=F32)


def mm_nt(a, b):
    return lax.dot_general(a, b, (((1,), (1,)), ((), ())), preferred_element_type=F32)


def add_into(ref, *others):
    total = ref[...].astype(F32)
    for other in others:
        total = total + other[...].astype(F32)
    ref[...] = total.astype(BF16)


def kernel(
    order, lat_in, nope_in, rope_in, gout_in, w_in,
    gn_far, gr_far, gl_far, gu_far,
    kbuf, keys, keys_t, nope_p, rope_p, gout_p, w_all, wk_t,
    query, grad, probs, gprob, gscore, peaks, peak, total, centre, stat_s, stat_r,
    dq_t, out_t, gn_own, gn_send, gn_recv, ro_recv,
    dkb, ra1, ra2, ra3, rb1, rb2, rb3,
    up, uc, uzs, uz, us2, uyr, us3, uxr,
    lat, nope_o, rope_o, gout_o, w_own, loads, gn_out, gr_out, gl_out, gu_out, stores,
    send, recv,
):
    f = lax.axis_index("fsdp")
    blk = lax.axis_index("blk")
    x, zl, y = blk % 4, (blk // 4) % 2, blk // 8
    xp, xm, x2 = (x + 1) % 4, (x + 3) % 4, (x + 2) % 4
    yp, ym, y2 = (y + 1) % 4, (y + 3) % 4, (y + 2) % 4
    f1 = f + 1 - 2 * (f % 2)
    f2 = (f + 2) % 4
    f3 = (f1 + 2) % 4
    pair_blk = blk + 4 - 8 * zl

    def at(yy, xx):
        return {"blk": (yy * 2 + zl) * 4 + xx}

    to_xp, to_xm, to_x2 = at(y, xp), at(y, xm), at(y, x2)
    to_yp, to_ym, to_y2 = at(yp, x), at(ym, x), at(y2, x)
    to_pair = {"blk": pair_blk}
    to_core = {"fsdp": f1}
    to_far = {"fsdp": f2, "blk": pair_blk}
    to_z2 = {"fsdp": f2}

    made = {}

    def define(name, src, dst, device):
        number = len(made)
        made[name] = lambda: pltpu.make_async_remote_copy(
            src_ref=src(), dst_ref=dst(), send_sem=send.at[number], recv_sem=recv.at[number],
            device_id=device, device_id_type=MESH,
        )

    def start(*names):
        for name in names:
            made[name]().start()

    def wait(*names):
        for name in names:
            made[name]().wait_recv()

    def same(name, part, device):
        define(name, part, part, device)

    for name, first, swap in (("a", 0, False), ("b", 288, True)):
        def part(dy, dx, first=first, swap=swap):
            if swap:
                dy, dx = dx, dy
            return lambda: kbuf.at[((y + dy) % 4) * 4 + (x + dx) % 4, pl.ds(first, 288)]

        if swap:
            ip, im, i2, jp, jm = to_yp, to_ym, to_y2, to_xp, to_xm
        else:
            ip, im, i2, jp, jm = to_xp, to_xm, to_x2, to_yp, to_ym
        same(name + "1", part(0, 0), ip)
        same(name + "2", part(0, 0), im)
        same(name + "5", part(0, 0), i2)
        same(name + "3", part(0, 0), jp)
        same(name + "4", part(0, 0), jm)
        same(name + "7", part(0, 3), jp)
        same(name + "8", part(0, 3), jm)
        same(name + "9", part(0, 1), jp)
        same(name + "10", part(0, 1), jm)
        same(name + "11", part(0, 2), jp)
        same(name + "12", part(0, 2), jm)
        same(name + "13", part(3, 0), jp)
        same(name + "14", part(3, 3), jp)
        same(name + "15", part(1, 1), jm)
        same(name + "16", part(1, 2), jm)

    define("qn", lambda: nope_o, lambda: nope_p, to_pair)
    define("qr", lambda: rope_o, lambda: rope_p, to_pair)
    define("qg", lambda: gout_o, lambda: gout_p, to_pair)
    for name, first in (("k", 0), ("v", 1024)):
        def own_w(first=first):
            return w_own.at[:, pl.ds(first, 1024)]

        def far_w(shard, first=first):
            return lambda: w_all.at[shard, :, pl.ds(first, 1024)]

        define(f"w{name}1", own_w, far_w(f), to_core)
        define(f"w{name}2", own_w, far_w(f), to_far)
        define(f"w{name}3", far_w(f2), far_w(f2), to_core)
    define("st0", lambda: stat_s.at[pl.ds(0, 2)], lambda: stat_r.at[pl.ds(2, 2)], to_pair)
    define("st1", lambda: stat_s.at[pl.ds(2, 2)], lambda: stat_r.at[pl.ds(0, 2)], to_pair)
    define("gn", lambda: gn_send, lambda: gn_recv, to_pair)
    define("ro0", lambda: dq_t.at[2, pl.ds(512, 64)], lambda: ro_recv.at[0], to_pair)
    define("ro1", lambda: dq_t.at[3, pl.ds(512, 64)], lambda: ro_recv.at[1], to_pair)

    def term(yy, xx, first):
        return lambda: dkb.at[yy, xx, pl.ds(first, 288)]

    def column(d):
        return (x + d) % 4

    for d in range(4):
        sign, device = ("p", to_yp) if d in (1, 2) else ("m", to_ym)
        define(f"A1{sign}{d}", term(y2, column(d), 0), lambda d=d: ra1.at[d], device)
        define(f"A2p{d}", term(yp, column(d), 0), lambda d=d: ra2.at[0, d], to_yp)
        define(f"A2m{d}", term(ym, column(d), 0), lambda d=d: ra2.at[1, d], to_ym)
    for d, device in ((1, to_xp), (2, to_x2), (3, to_xm)):
        define(f"A3{d}", term(y, column(d), 0), lambda d=d: ra3.at[d - 1], device)
    turns = (y2, yp, ym, y)
    for i in range(4):
        define(f"B1{i}", term(turns[i], x2, 288), lambda i=i: rb1.at[i], to_x2)
        define(f"B2p{i}", term(turns[i], xp, 288), lambda i=i: rb2.at[i, 0], to_xp)
        define(f"B2m{i}", term(turns[i], xm, 288), lambda i=i: rb2.at[i, 1], to_xm)
    for i, device in enumerate((to_y2, to_yp, to_ym)):
        define(f"B3{i}", term(turns[i], x, 288), lambda i=i: rb3.at[i], device)

    for i in range(4):
        define(f"C0{i}", lambda i=i: up.at[i, f1], lambda i=i: uc.at[i, 0], to_core)
        define(f"C1{i}", lambda i=i: up.at[i, f3], lambda i=i: uc.at[i, 1], to_core)
        for j, device in enumerate((to_pair, to_far, to_z2)):
            define(f"Z{j}{i}", lambda i=i, j=j: uzs.at[i, j], lambda i=i, j=j: uz.at[i, j], device)
        for j, (yy, device) in enumerate(((yp, to_yp), (ym, to_ym), (y2, to_y2))):
            define(f"Y{j}{i}", lambda i=i, yy=yy: us2.at[i, yy], lambda i=i, j=j: uyr.at[i, j], device)
        for j, device in enumerate((to_xp, to_xm, to_x2)):
            define(f"X{j}{i}", lambda i=i: us3.at[i], lambda i=i, j=j: uxr.at[i, j], device)

    barrier = pltpu.get_barrier_semaphore()
    partners = (to_xp, to_xm, to_x2, to_yp, to_ym, to_y2, to_pair, to_core, to_far, to_z2)
    for partner in partners:
        pl.semaphore_signal(barrier, inc=1, device_id=partner, device_id_type=MESH)
    pairs = ((w_in, w_own), (nope_in, nope_o), (lat_in, lat), (rope_in, rope_o), (gout_in, gout_o))
    copies = [pltpu.make_async_copy(source, target, loads.at[i]) for i, (source, target) in enumerate(pairs)]
    for copy in copies:
        copy.start()
    query[:, 512:640, :] = jnp.zeros((4, 128, 512), BF16)
    keys[:, :, 512:640] = jnp.zeros((8, 256, 128), BF16)
    for copy in copies:
        copy.wait()
    kbuf[y * 4 + x] = lat[...]
    w_all[f] = w_own[...]
    pl.semaphore_wait(barrier, len(partners))

    start("wk2", "qn", "wv2", "a1", "b1", "a2", "b2", "a5", "b5", "a3", "b3", "a4", "b4", "qr", "wk1")

    def place_rope(rope, s):
        for k in range(4):
            turned = jnp.transpose(rope[:, k * 128 : k * 128 + 128].astype(F32))
            lanes = slice(k * 128, k * 128 + 128)
            query[2 * s + 1, 512:576, lanes] = jnp.concatenate([turned[:64, :64], turned[64:, :64]], axis=1).astype(BF16)
            query[2 * s, 512:576, lanes] = jnp.concatenate([turned[:64, 64:], turned[64:, 64:]], axis=1).astype(BF16)

    place_rope(rope_o, 0)
    for name in ("a", "b"):
        wait(name + "1")
        start(name + "7", name + "8")
    for name in ("a", "b"):
        wait(name + "2")
        start(name + "9", name + "10")
    for name in ("a", "b"):
        wait(name + "5")
        start(name + "11", name + "12")
    start("qg", "wv1")
    for name in ("a", "b"):
        wait(name + "3")
        start(name + "13")
    wait("wk2")
    start("wk3")
    for name in ("a", "b"):
        wait(name + "7")
        start(name + "14")
    for name in ("a", "b"):
        wait(name + "10")
        start(name + "15")
    for name in ("a", "b"):
        wait(name + "12")
        start(name + "16")

    def blocks(value, lanes):
        both = value[:, lanes]
        empty = jnp.zeros((64, 128), BF16)
        rows = []
        for half in (both[:64], both[64:]):
            rows.append(jnp.concatenate([half[:, :128], empty], axis=1))
            rows.append(jnp.concatenate([empty, half[:, 128:]], axis=1))
        return jnp.concatenate(rows, axis=0)

    def project(value, first, ref, s):
        def two_heads(k, _):
            lanes = pl.ds(pl.multiple_of(k * 256, 256), 256)
            w_lanes = pl.ds(pl.multiple_of(first + k * 256, 256), 256)
            to = pl.ds(pl.multiple_of(k * 128, 128), 128)
            out = mm_nt(w_all[:, :, w_lanes].reshape(512, 256), blocks(value, lanes)).astype(BF16)
            ref[2 * s + 1, 0:512, to] = out[:, :128]
            ref[2 * s, 0:512, to] = out[:, 128:]
            return 0

        lax.fori_loop(0, 4, two_heads, 0)

    wait("wk1", "wk3")
    wait("wv2")
    start("wv3")
    project(nope_o, 0, query, 0)
    for s in range(4):
        wk_t[:, s * 128 : s * 128 + 128] = jnp.transpose(w_all[s, :, 0:1024])
    wait("qn", "qr")
    place_rope(rope_p, 1)
    project(nope_p, 0, query, 1)

    def assemble(yy, xx):
        both = [kbuf[yy * 4 + xx + j] for j in range(2)]
        lanes = pl.ds(pl.multiple_of(yy * 256 + xx * 64, 128), 128)
        high_lanes = pl.ds(pl.multiple_of(1024 + yy * 256 + xx * 64, 128), 128)
        keys_t[:, lanes] = jnp.concatenate([b[:, :64] for b in both], axis=1)
        keys_t[:, high_lanes] = jnp.concatenate([b[:, 64:] for b in both], axis=1)
        for j in range(2):
            rows = slice((xx + j) * 64, (xx + j) * 64 + 64)
            main = jnp.transpose(both[j][:512])
            rest = jnp.transpose(both[j][512:])
            keys[yy, rows, 0:512] = main[:64]
            keys[yy, rows, 512:576] = rest[:64]
            keys[4 + yy, rows, 0:512] = main[64:]
            keys[4 + yy, rows, 512:576] = rest[64:]

    def key_row(yy, *names):
        wait(*names)
        assemble(yy, 0)
        assemble(yy, 2)

    key_row(y, "b4", "b13")
    key_row(yp, "a4", "a8", "b9", "b15")
    key_row(ym, "a9", "a11", "b8", "b14")
    wait("wv1", "wv3")
    project(gout_o, 1024, grad, 0)
    peak[...] = jnp.full((4, 1, 512), NEG_START, F32)
    total[...] = jnp.zeros((4, 1, 512), F32)
    centre[...] = jnp.zeros((4, 1, 512), F32)
    relative = lax.broadcasted_iota(jnp.int32, (64, 512), 0) - lax.broadcasted_iota(jnp.int32, (64, 512), 1) % 64

    def visit(t, g, high, masked, first):
        tile = 4 + t if high else t
        slot = 16 + (g // 2) * 4 + t if high else g * 4 + t
        scores = mm(keys[tile], query[g])
        grad_probs = mm(keys[tile, :, 0:512], grad[g])
        if masked:
            block = 63 - first if high else first
            parts = []
            for xx in range(4):
                key_first = order[0, (t * 2 + zl) * 4 + xx]
                key_block = 63 - key_first if high else key_first
                parts.append(relative <= (block - key_block) * 64)
            scores = jnp.where(jnp.concatenate(parts, axis=0), scores, NEG_FILL)
        old = peak[g]
        new = jnp.maximum(old, jnp.max(scores, axis=0, keepdims=True))
        weights = jnp.exp2((scores - new) * BASE2)
        factor = jnp.exp2((old - new) * BASE2)
        total[g] = total[g] * factor + jnp.sum(weights, axis=0, keepdims=True)
        centre[g] = centre[g] * factor + jnp.sum(weights * grad_probs, axis=0, keepdims=True)
        peak[g] = new
        probs[slot] = weights.astype(BF16)
        gprob[slot] = grad_probs
        peaks[slot] = new

    def visits(s, first, begin, end):
        def step(i, _):
            t = (y + jnp.where(i == 0, 0, jnp.where(i == 1, 1, jnp.where(i == 2, 3, 2)))) % 4
            visit(t, 2 * s, False, False, first)
            visit(t, 2 * s + 1, False, True, first)
            visit(t, 2 * s, True, True, first)
            return 0

        lax.fori_loop(begin, end, step, 0)

    def tell(s):
        for g in (2 * s, 2 * s + 1):
            stat_s[g, 0:1] = peak[g]
            stat_s[g, 1:2] = total[g]
            stat_s[g, 2:3] = centre[g]
        start(f"st{s}")

    visits(0, order[0, blk], 0, 3)
    key_row(y2, "a13", "a14", "a15", "a16", "b11", "b16")
    visits(0, order[0, blk], 3, 4)
    tell(0)
    wait("qg")
    project(gout_p, 1024, grad, 1)
    visits(1, order[0, pair_blk], 0, 4)
    tell(1)

    def normalise(slot, g):
        factor = jnp.exp2((peaks[slot] - peak[g]) * BASE2) / total[g]
        p = probs[slot].astype(F32) * factor
        probs[slot] = p.astype(BF16)
        gscore[slot] = (p * (gprob[slot] - centre[g]) * SCALE).astype(BF16)

    def merge(s):
        wait(f"st{1 - s}")
        for g in (2 * s, 2 * s + 1):
            here, there = stat_s[g], stat_r[g]
            new = jnp.maximum(here[0:1], there[0:1])
            f_here = jnp.exp2((here[0:1] - new) * BASE2)
            f_there = jnp.exp2((there[0:1] - new) * BASE2)
            norm = here[1:2] * f_here + there[1:2] * f_there
            peak[g] = new
            total[g] = norm
            centre[g] = (here[2:3] * f_here + there[2:3] * f_there) / norm

        def low_slots(i, _):
            normalise(s * 8 + i, 2 * s + i // 4)
            return 0

        def high_slots(i, _):
            normalise(16 + s * 4 + i, 2 * s)
            return 0

        lax.fori_loop(0, 8, low_slots, 0)
        lax.fori_loop(0, 4, high_slots, 0)

    def times_keys(ref, rows, source, s, lanes):
        low = source[8 * s : 8 * s + 4, :, lanes].reshape(1024, -1)
        high = source[16 + 4 * s : 20 + 4 * s, :, lanes].reshape(1024, -1)
        ref[2 * s, :, lanes] = mm(keys_t[rows, :], jnp.concatenate([low, high], axis=0)).astype(BF16)
        low = source[8 * s + 4 : 8 * s + 8, :, lanes].reshape(1024, -1)
        ref[2 * s + 1, :, lanes] = mm(keys_t[rows, 0:1024], low).astype(BF16)

    def two_heads_rows(own, pair, k):
        lanes = slice(k * 256, k * 256 + 256)
        mine, other = blocks(own, lanes), blocks(pair, lanes)
        return jnp.concatenate([mine[128:], mine[:128], other[128:], other[:128]], axis=0)

    def weight_terms(i, ref, own, pair):
        for j in range(2):
            k = (i % 2) * 2 + j
            left = jnp.concatenate([ref[g, 0:512, k * 128 : k * 128 + 128] for g in range(4)], axis=1)
            whole = mm(left, two_heads_rows(own, pair, k))
            up[i, :, :, j * 256 : j * 256 + 256] = whole.astype(BF16).reshape(4, 128, 256)
        start(f"C0{i}", f"C1{i}")

    def sum_core(i):
        wait(f"C0{i}", f"C1{i}")
        for j, (shard, slot, plane) in enumerate(((f, 0, 1 - zl), (f2, 1, 1 - zl), (f2, 1, zl))):
            for yy in range(4):
                rows = pl.ds(pl.multiple_of(yy * 32 + plane * 16, 16), 16)
                whole = up[i, shard, rows].astype(F32) + uc[i, slot, rows].astype(F32)
                uzs[i, j, yy] = whole.astype(BF16)
        start(f"Z0{i}", f"Z1{i}", f"Z2{i}")

    def sum_z(i):
        wait(f"Z0{i}", f"Z1{i}", f"Z2{i}")
        for yy in range(4):
            rows = pl.ds(pl.multiple_of(yy * 32 + zl * 16, 16), 16)
            whole = up[i, f, rows].astype(F32) + uc[i, 0, rows].astype(F32)
            for j in range(3):
                whole = whole + uz[i, j, yy].astype(F32)
            us2[i, yy] = whole.astype(BF16)
        start(f"Y0{i}", f"Y1{i}", f"Y2{i}")

    def sum_y(i):
        wait(f"Y0{i}", f"Y1{i}", f"Y2{i}")
        whole = us2[i, y].astype(F32) + uyr[i, 0].astype(F32) + uyr[i, 1].astype(F32) + uyr[i, 2].astype(F32)
        us3[i] = whole.astype(BF16)
        start(f"X0{i}", f"X1{i}", f"X2{i}")

    def sum_x(i):
        wait(f"X0{i}", f"X1{i}", f"X2{i}")
        whole = us3[i].astype(F32) + uxr[i, 0].astype(F32) + uxr[i, 1].astype(F32) + uxr[i, 2].astype(F32)
        mine_rows = whole[0:4]
        for xx in range(1, 4):
            mine_rows = jnp.where(x == xx, whole[xx * 4 : xx * 4 + 4], mine_rows)
        first = (1024, 1536, 0, 512)[i]
        gu_out[:, first : first + 512] = mine_rows

    def back(s, ref):
        def two_heads(k, _):
            lanes = pl.ds(pl.multiple_of(k * 128, 128), 128)
            rows = pl.ds(pl.multiple_of(k * 256, 256), 256)
            left = jnp.concatenate([dq_t[2 * s + 1, 0:512, lanes], dq_t[2 * s, 0:512, lanes]], axis=1)
            out = mm(wk_t[rows, :], left)
            ref[pl.ds(pl.multiple_of(k * 256, 256), 128), :] = jnp.concatenate(
                [out[:128, 0:64], out[:128, 128:192]], axis=1
            ).astype(ref.dtype)
            ref[pl.ds(pl.multiple_of(k * 256 + 128, 128), 128), :] = jnp.concatenate(
                [out[128:, 64:128], out[128:, 192:256]], axis=1
            ).astype(ref.dtype)
            return 0

        lax.fori_loop(0, 4, two_heads, 0)

    def key_tile(t):
        def one(slots):
            a = sum(mm_nt(query[g, 0:576], gscore[slot]) for g, slot in slots)
            b = sum(mm_nt(grad[g], probs[slot]) for g, slot in slots)
            return a[:512] + b, a[512:]

        low, low_rest = one([(g, g * 4 + t) for g in range(4)])
        high, high_rest = one([(2 * s, 16 + s * 4 + t) for s in range(2)])
        for xx in range(4):
            lanes = slice(xx * 64, xx * 64 + 64)
            dkb[t, xx, 0:512] = jnp.concatenate([low[:, lanes], high[:, lanes]], axis=1).astype(BF16)
            dkb[t, xx, 512:576] = jnp.concatenate([low_rest[:, lanes], high_rest[:, lanes]], axis=1).astype(BF16)

    upper, lower = pl.ds(0, 288), pl.ds(288, 288)

    def b_first(i):
        start(f"B1{i}", f"B2p{i}", f"B2m{i}")

    def b_last(i):
        wait(f"B1{i}", f"B2p{i}", f"B2m{i}")
        add_into(dkb.at[turns[i], x, lower], rb1.at[i], rb2.at[i, 0], rb2.at[i, 1])
        start(f"B3{i}")

    every, halves = slice(0, 512), (slice(0, 256), slice(256, 512))
    main, full = slice(0, 512), slice(0, 576)
    def a_second(d, row, sign):
        wait(f"A1{sign}{d}")
        add_into(dkb.at[row, column(d), upper], ra1.at[d])
        start(f"A2{sign}{d}")

    merge(1)
    times_keys(out_t, main, probs, 1, every)
    merge(0)

    def first_turn(i, _):
        key_tile((y + 2 - i) % 4)

        @pl.when(i == 0)
        def _():
            start("A1p2", "A1m3", "A1p1", "A1m0")
            b_first(0)

        return 0

    lax.fori_loop(0, 2, first_turn, 0)
    start("A2p3", "A2p0")
    b_first(1)
    times_keys(dq_t, full, gscore, 1, every)
    back(1, gn_send)
    start("ro0", "ro1", "gn")
    a_second(2, yp, "p")
    a_second(1, yp, "p")
    times_keys(out_t, main, probs, 0, halves[0])
    weight_terms(0, out_t, gout_o, gout_p)
    times_keys(out_t, main, probs, 0, halves[1])
    weight_terms(1, out_t, gout_o, gout_p)
    sum_core(0)
    b_last(0)
    times_keys(dq_t, full, gscore, 0, halves[0])
    weight_terms(2, dq_t, nope_o, nope_p)
    sum_core(1)
    times_keys(dq_t, full, gscore, 0, halves[1])
    weight_terms(3, dq_t, nope_o, nope_p)
    sum_core(2)
    b_last(1)

    def key_turn(i, _):
        key_tile((y + jnp.where(i == 2, 3, 0)) % 4)

        @pl.when(i == 2)
        def _():
            start("A2m2", "A2m1")
            b_first(2)
            sum_core(3)
            a_second(3, ym, "m")
            a_second(0, ym, "m")
            sum_z(0)
            sum_z(1)

        return 0

    lax.fori_loop(2, 4, key_turn, 0)
    b_first(3)

    def a_last(d):
        wait(f"A2p{d}", f"A2m{d}")
        add_into(dkb.at[y, column(d), upper], ra2.at[0, d], ra2.at[1, d])
        start(f"A3{d}")

    sum_z(2)
    a_last(2)
    sum_z(3)
    a_last(1)
    a_last(3)
    b_last(2)
    sum_y(0)
    sum_y(1)
    sum_y(2)
    sum_y(3)
    back(0, gn_own)
    sum_x(0)
    sum_x(1)

    wait("gn", "ro0", "ro1")
    gn_out[...] = jnp.transpose(gn_own[...] + gn_recv[...].astype(F32)).astype(BF16)
    for half, g in ((0, 1), (1, 0)):
        rope = jnp.transpose(dq_t[g, 512:576].astype(F32) + ro_recv[g].astype(F32))
        gr_out[half * 64 : half * 64 + 64, :] = jnp.concatenate(
            [rope[h * 64 : h * 64 + 64] for h in range(HEADS)], axis=1
        ).astype(BF16)

    pairs = ((gn_out, gn_far), (gr_out, gr_far), (gl_out, gl_far), (gu_out, gu_far))
    leave = [pltpu.make_async_copy(source, target, stores.at[i]) for i, (source, target) in enumerate(pairs)]
    leave[0].start()
    leave[1].start()
    wait("A31", "A32", "A33", "A2p0", "A2m0")
    add_into(dkb.at[y, x, upper], ra2.at[0, 0], ra2.at[1, 0], ra3.at[0], ra3.at[1], ra3.at[2])
    wait("B13", "B2p3", "B2m3", "B30", "B31", "B32")
    add_into(dkb.at[y, x, lower], rb1.at[3], rb2.at[3, 0], rb2.at[3, 1], rb3.at[0], rb3.at[1], rb3.at[2])
    gl_out[...] = dkb[y, x]
    leave[2].start()
    sum_x(2)
    sum_x(3)
    leave[3].start()
    for name in made:
        made[name]().wait_send()
    for copy in leave:
        copy.wait()


def hand_over(*refs):
    for source, target in zip(refs[:4], refs[4:]):
        target[...] = source[...]


def per_device(query_nope, query_rope, latent, grad_out, w_up, block_order):
    shapes = [
        ((16, 576, 128), BF16), ((8, 256, 640), BF16), ((576, 2048), BF16),
        ((128, 1024), BF16), ((128, 512), BF16), ((128, 1024), BF16), ((4, 128, 2048), BF16), ((1024, 512), BF16),
        ((4, 640, 512), BF16), ((4, 512, 512), BF16), ((24, 256, 512), BF16), ((24, 256, 512), F32), ((24, 256, 512), BF16),
        ((24, 1, 512), F32), ((4, 1, 512), F32), ((4, 1, 512), F32), ((4, 1, 512), F32), ((4, 8, 512), F32), ((4, 8, 512), F32),
        ((4, 576, 512), BF16), ((4, 512, 512), BF16), ((1024, 128), F32), ((1024, 128), BF16), ((1024, 128), BF16), ((2, 64, 512), BF16),
        ((4, 4, 576, 128), BF16), ((4, 288, 128), BF16), ((2, 4, 288, 128), BF16), ((3, 288, 128), BF16),
        ((4, 288, 128), BF16), ((4, 2, 288, 128), BF16), ((3, 288, 128), BF16),
        ((4, 4, 128, 512), BF16), ((4, 2, 128, 512), BF16), ((4, 3, 4, 16, 512), BF16), ((4, 3, 4, 16, 512), BF16),
        ((4, 4, 16, 512), BF16), ((4, 3, 16, 512), BF16), ((4, 16, 512), BF16), ((4, 3, 16, 512), BF16),
        ((576, 128), BF16), ((128, 1024), BF16), ((128, 512), BF16), ((128, 1024), BF16), ((128, 2048), BF16),
    ]
    vmem = pl.BlockSpec(memory_space=pltpu.VMEM)
    gn, gr, gl, gu = pl.pallas_call(
        kernel,
        out_shape=(
            jax.ShapeDtypeStruct((128, 1024), BF16),
            jax.ShapeDtypeStruct((128, 512), BF16),
            jax.ShapeDtypeStruct((576, 128), BF16),
            jax.ShapeDtypeStruct((4, 2048), F32),
        ),
        in_specs=[pl.BlockSpec(memory_space=pltpu.SMEM)] + [pl.BlockSpec(memory_space=pl.ANY)] * 5,
        out_specs=(pl.BlockSpec(memory_space=pl.ANY),) * 4,
        scratch_shapes=[pltpu.VMEM(shape, dtype) for shape, dtype in shapes]
        + [pltpu.SemaphoreType.DMA((5,))]
        + [pltpu.VMEM((128, 1024), BF16), pltpu.VMEM((128, 512), BF16), pltpu.VMEM((576, 128), BF16), pltpu.VMEM((4, 2048), F32)]
        + [pltpu.SemaphoreType.DMA((4,)), pltpu.SemaphoreType.DMA((COPIES,)), pltpu.SemaphoreType.DMA((COPIES,))],
        compiler_params=pltpu.CompilerParams(
            collective_id=0, has_side_effects=True, vmem_limit_bytes=63 * 1024 * 1024
        ),
        name="latent_attention_backward",
    )(block_order.T, latent[0].T, query_nope[0], query_rope[0], grad_out[0], w_up)
    gn, gr, gl, gu = pl.pallas_call(
        hand_over,
        out_shape=tuple(jax.ShapeDtypeStruct(a.shape, a.dtype) for a in (gn, gr, gl, gu)),
        in_specs=[vmem] * 4,
        out_specs=(vmem,) * 4,
        name="hand_over",
    )(gn, gr, gl, gu)
    return gn[None], gr[None], gl.T[None], gu


def solution(mesh):
    rows = P("fsdp", "blk", None)
    return jax.shard_map(
        per_device,
        mesh=mesh,
        in_specs=(rows, rows, rows, rows, P("fsdp", None), P()),
        out_specs=(rows, rows, rows, P(("fsdp", "blk"), None)),
        check_vma=False,
    )
```
